256 devices in a mesh: dp: 16 (over z, core), camp: 16 (over x, y).
Axes of the slice: x: 4, y: 4, z: 8, core: 2. Of those that a mesh axis runs over, the one named last changes fastest.
Arguments:
- row_factors: bfloat16 [131072, 32], P('dp'), may hold values from -120 to 120
- col_factors: bfloat16 [1048576, 32], P('camp'), may hold values from -1 to 1
- prices: float32 [1048576], P('camp'), may hold values from 0.05 to 1
- spend_target: float32 [1048576], P('camp'), may hold values from 0.01 to 0.3
- step_sizes: float32 [3], replicated, may hold values from 1 to 4
- eligible: int32 [1024, 32], P('dp'), may hold values from 0 to 8191, as said below
- counts: int32 [1024], P('dp'), may hold values from 16 to 32
Outputs:
- new_prices: float32 [1048576], P('camp')
- row_norms: float32 [131072], P('dp')
The draws below stay inside these ranges and needn't reach their ends.
Inputs may be any that keep to these rules, and one draw needn't show every extreme that they name: `eligible`: each row block's slots are grouped by owning camp shard (column block // 512), each shard's slots contiguous, the shards in cyclic order; the first group belongs to the row block's leading shard and holds exactly 8 slots, every later group at most 2, and some later group exactly 2; the column blocks of a row block are distinct. Within each aligned run of 64 row blocks one camp shard leads exactly 8 row blocks and no shard leads more.
All inputs are finite; a program needn't handle non-finite values.
Results may differ from the reference program's by a relative error of at most 0.0006.
Values sent between devices are 32-bit elements; how exact they have to be, the bound alone decides.
A program may use at most 64 MiB of HBM per device.

```python
import math
import jax
import jax.numpy as jnp
import numpy as np
from jax import lax

BLOCK = 128
R = 32
SLOTS = 32
SHARD_MOST = 8
PASSES = 3
CB_DEV = 512
RB_DEV = 64
LEAD_MOST = 8
ROW_BLOCKS = 1024
CAMPAIGNS = 1048576
N_DP = 16
N_CAMP = 16


def draw_row_factors(key, part):
    key = jax.random.fold_in(key, 5)
    first_key = jax.random.fold_in(key, 0)
    values = jnp.clip(jax.random.normal(first_key, (RB_DEV * N_DP * BLOCK, R), jnp.float32), -4.0, 4.0)
    return values.astype(jnp.bfloat16)


def draw_eligible(key, part):
    key = jax.random.fold_in(key, 7)
    keys = jax.random.split(key, 5)
    total_blocks = RB_DEV * N_DP
    start_shard = jax.random.randint(keys[0], (N_DP,), 0, N_CAMP)
    turn_list = [0] * LEAD_MOST + [1 + (b - LEAD_MOST) % (N_CAMP - 1) for b in range(LEAD_MOST, RB_DEV)]
    turn_table = jnp.asarray(np.array(turn_list, dtype=np.int32))
    orders = jax.vmap(lambda k: jax.random.permutation(k, RB_DEV))(jax.random.split(keys[1], N_DP))
    leading = ((start_shard[:, None] + turn_table[orders]) % N_CAMP).reshape(total_blocks)
    remain = SLOTS - SHARD_MOST
    quotient = remain // (N_CAMP - 1)
    extra = remain % (N_CAMP - 1)
    group_sizes = [SHARD_MOST] + [quotient + (1 if r < extra else 0) for r in range(N_CAMP - 1)]
    rotation = np.repeat(np.arange(N_CAMP), group_sizes)[:SLOTS].astype(np.int32)
    ranking = np.concatenate([np.arange(g) for g in group_sizes])[:SLOTS].astype(np.int32)
    shard = (leading[:, None] + jnp.asarray(rotation)[None, :]) % N_CAMP
    base = jax.random.randint(keys[3], (total_blocks, N_CAMP), 0, CB_DEV)
    stride = 2 * jax.random.randint(keys[4], (total_blocks, N_CAMP), 0, max(CB_DEV // 2, 1)) + 1
    base_slot = jnp.take_along_axis(base, shard, axis=1)
    stride_slot = jnp.take_along_axis(stride, shard, axis=1)
    local_block = (base_slot + jnp.asarray(ranking)[None, :] * stride_slot) % CB_DEV
    return (shard * CB_DEV + local_block).astype(jnp.int32)


def touch_ends(values, own_key, least, largest):
    longest = values.shape.index(max(values.shape))
    spots = []
    for shift in (0, 1):
        where = [jax.random.randint(jax.random.fold_in(own_key, axis), (), 0, length) for axis, length in enumerate(values.shape)]
        where[longest] = (where[longest] + shift) % values.shape[longest]
        spots.append(tuple(where))
    return values.at[spots[0]].set(least).at[spots[1]].set(largest)


def levels(key, shape, cuts, smallest, high):
    factor_of = 1.0
    for position, shards_of in cuts:
        draws = jax.random.uniform(jax.random.fold_in(jax.random.fold_in(key, 6), position), (shards_of,), jnp.float32, smallest / len(cuts), high / len(cuts))
        factor_of = factor_of * jnp.repeat(jnp.exp(draws), shape[position] // shards_of).reshape((-1,) + (1,) * (len(shape) - 1 - position))
    return factor_of


def gaussian(own_key, dims, spread, bound, shards=(), kind=jnp.bfloat16):
    drawn = spread * jax.random.normal(own_key, dims, jnp.float32)
    if shards:
        drawn = drawn * levels(own_key, dims, shards, -0.22, 0.18)
    return jnp.clip(drawn, -bound, bound).astype(kind)


def setup_inputs(seed: int = 0) -> dict:
    key_list = jax.random.split(jax.random.key(seed), 8)
    return {
        "row_factors": draw_row_factors(jax.random.fold_in(key_list[7], 71), 0),
        "col_factors": gaussian(key_list[1], (CAMPAIGNS, R), R ** -0.5, 1.0, ((0, 16),)),
        "prices": jnp.clip(jnp.exp(math.log(1.0) - 2.9957323 * jax.random.uniform(key_list[2], (CAMPAIGNS,), jnp.float32) ** levels(key_list[2], (CAMPAIGNS,), ((0, 16),), -0.2, 0.2)), 0.05, 1.0),
        "spend_target": jnp.clip(jnp.exp(math.log(0.3) - 3.4011974 * jax.random.uniform(key_list[3], (CAMPAIGNS,), jnp.float32) ** levels(key_list[3], (CAMPAIGNS,), ((0, 16),), -0.2, 0.2)), 0.01, 0.3),
        "step_sizes": jnp.clip(jnp.exp(jax.random.uniform(key_list[4], (PASSES,), jnp.float32, math.log(1.0), math.log(4.0))), 1.0, 4.0),
        "eligible": draw_eligible(jax.random.fold_in(key_list[7], 71), 0),
        "counts": touch_ends(jax.random.randint(key_list[6], (ROW_BLOCKS,), SLOTS // 2, SLOTS + 1), jax.random.fold_in(key_list[6], 1), SLOTS // 2, SLOTS).astype(jnp.int32),
    }


SMOOTHING_TEMP = 0.3


def reference(row_factors, col_factors, prices, spend_target, step_sizes, eligible, counts):
    total_blocks = RB_DEV * N_DP
    group = math.gcd(total_blocks, 16)
    steps_count = total_blocks // group
    row_tiles = row_factors.astype(jnp.float32).reshape(steps_count, group, BLOCK, R)
    slot_ids = eligible.reshape(steps_count, group, SLOTS)
    slot_counts = counts.reshape(steps_count, group)
    col_tiles = col_factors.astype(jnp.float32).reshape(CB_DEV * N_CAMP, BLOCK, R)
    slot_index = jnp.arange(SLOTS, dtype=jnp.int32)
    price = prices
    norms = None
    for pass_index in range(PASSES):
        price_pieces = price.reshape(CB_DEV * N_CAMP, BLOCK)

        def visit(carry, item):
            rows, group_identifiers, count_group = item
            live = slot_index[None, :] < count_group[:, None]
            gathered = col_tiles[group_identifiers]
            score_values = jnp.einsum("grk,gsck->gsrc", rows, gathered, precision=lax.Precision.HIGHEST)
            logit_values = (score_values - price_pieces[group_identifiers][:, :, None, :]) / SMOOTHING_TEMP
            live_mask = live[:, :, None, None]
            top_value = jnp.maximum(jnp.max(jnp.where(live_mask, logit_values, -jnp.inf), axis=(1, 3)), 0.0)
            sum_value = jnp.sum(jnp.where(live_mask, jnp.exp(logit_values - top_value[:, None, :, None]), 0.0), axis=(1, 3))
            log_norm = top_value + jnp.log(sum_value + jnp.exp(-top_value))
            assign = jnp.where(live_mask, jnp.exp(logit_values - log_norm[:, None, :, None]), 0.0)
            col_part = jnp.sum(assign, axis=2)
            carry = carry.at[group_identifiers.reshape(-1)].add(col_part.reshape(-1, BLOCK))
            return carry, log_norm

        start = jnp.zeros((CB_DEV * N_CAMP, BLOCK), jnp.float32)
        colsum, norms = lax.scan(visit, start, (row_tiles, slot_ids, slot_counts))
        price = jnp.maximum(price + step_sizes[pass_index] * (colsum.reshape(-1) - spend_target), 0.0)
    return price, norms.reshape(-1)
```

```python
import functools
import math

import jax
import jax.numpy as jnp
from jax import lax
from jax.experimental import pallas as pl
from jax.experimental.pallas import tpu as pltpu
from jax.sharding import PartitionSpec as P

MESH = pl.DeviceIdType.MESH
F32 = jnp.float32
BF16 = jnp.bfloat16
BLOCK = 128
RANK = 32
PASSES = 3
LEADS = 8
LEAD_SLOTS = 8
SCALE = math.log2(math.e) / 0.3
LN2 = math.log(2.0)
DEAD = 1e30
GROUP = 4


def pieces(x):
    hi = x.astype(BF16)
    rest = x - hi.astype(F32)
    mid = rest.astype(BF16)
    low = (rest - mid.astype(F32)).astype(BF16)
    return hi, mid, low


def mm(a, b):
    return lax.dot_general(a, b, (((1,), (0,)), ((), ())), preferred_element_type=F32)


def mm_nt(a, b):
    return lax.dot_general(a, b, (((1,), (1,)), ((), ())), preferred_element_type=F32)


def exact_pick(select, x):
    hi, mid, low = pieces(x)
    out = mm(select, jnp.concatenate([hi, mid, low], axis=1))
    return out[:, :BLOCK] + out[:, BLOCK : 2 * BLOCK] + out[:, 2 * BLOCK :]


def slot_index(elig, cnt, own, col_blocks):
    slots, rows = elig.shape
    pos = lax.broadcasted_iota(jnp.int32, elig.shape, 0)
    owned = lax.div(elig, col_blocks) == own
    led = owned[0:1, :]
    first = jnp.min(jnp.where(owned, pos, slots), axis=0, keepdims=True)
    blocks, valids = [], []
    for k in range(2):
        picked = first + k
        chosen = jnp.sum(jnp.where(pos == picked, elig, 0), axis=0, keepdims=True)
        ok = (
            (picked < slots)
            & (lax.div(chosen, col_blocks) == own)
            & (picked < cnt)
            & jnp.logical_not(led)
        )
        blocks.append(jnp.where(ok, chosen - own * col_blocks, 0))
        valids.append(ok.astype(jnp.int32))
    led_f = jnp.broadcast_to(led.astype(F32), (8, rows))
    before = (
        lax.broadcasted_iota(jnp.int32, (rows, rows), 0)
        < lax.broadcasted_iota(jnp.int32, (rows, rows), 1)
    ).astype(F32)
    rank = mm(led_f.astype(BF16), before.astype(BF16))[0:1, :]
    lane = lax.broadcasted_iota(jnp.int32, (LEADS * LEAD_SLOTS, rows), 0)
    hot = jnp.where((rank == lax.rem(lane, LEADS).astype(F32)) & led, 1.0, 0.0)
    row_id = lax.broadcasted_iota(jnp.int32, (8, rows), 1).astype(F32)
    high = lax.div(elig, 128)
    picked = mm_nt(
        jnp.concatenate(
            [
                high.astype(F32),
                (elig - high * 128).astype(F32),
                jnp.broadcast_to(cnt, (8, rows)).astype(F32),
                jnp.ones((8, rows), F32),
                row_id,
            ],
            axis=0,
        ).astype(BF16),
        hot.astype(BF16),
    )
    wide = LEADS * LEAD_SLOTS
    every = picked[0:slots] * 128.0 + picked[slots : 2 * slots]
    slot_of = lax.div(lax.broadcasted_iota(jnp.int32, (slots, wide), 1), LEADS)
    chosen = jnp.sum(
        jnp.where(lax.broadcasted_iota(jnp.int32, (slots, wide), 0) == slot_of, every, 0.0),
        axis=0,
        keepdims=True,
    ).astype(jnp.int32)
    lead_cnt = picked[2 * slots : 2 * slots + 1]
    exists = picked[2 * slots + 8 : 2 * slots + 9] > 0.5
    lead_row = picked[2 * slots + 16 : 2 * slots + 17].astype(jnp.int32)
    ok = exists & (slot_of[0:1].astype(F32) < lead_cnt)
    blocks.append(jnp.where(ok, chosen - own * col_blocks, 0))
    valids.append(ok.astype(jnp.int32))
    blocks.append(jnp.zeros_like(lead_row))
    valids.append(jnp.zeros_like(lead_row))
    place = jnp.where(exists, lead_row, -1)
    return (
        jnp.concatenate(blocks, axis=1),
        jnp.concatenate(valids, axis=1),
        jnp.concatenate([lead_row, place, lead_row, place], axis=1),
    )


def gather_kernel(
    col_blocks,
    elig_ref,
    cnt_ref,
    row_ref,
    col_ref,
    index_out,
    tiles_out,
    lead_tiles_out,
    lead_rows_out,
    col_vmem,
    index_s,
    sem,
):
    load = pltpu.make_async_copy(col_ref, col_vmem, sem.at[0])
    load.start()
    own = lax.axis_index("camp")
    block_id, valid, lead_info = slot_index(elig_ref[...], cnt_ref[...], own, col_blocks)
    rest = jnp.zeros((5, block_id.shape[1]), jnp.int32)
    index_out[...] = jnp.concatenate([block_id, valid, lead_info, rest], axis=0)
    to_smem = pltpu.make_async_copy(index_out, index_s, sem.at[1])
    to_smem.start()
    to_smem.wait()
    load.wait()
    row_blocks = tiles_out.shape[0]

    def pick(t):
        return col_vmem[:, pl.ds(pl.multiple_of(index_s[0, t] * BLOCK, BLOCK), BLOCK)]

    def regular(b, _):
        tiles_out[b, :, 0:BLOCK] = pick(b)
        tiles_out[b, :, BLOCK : 2 * BLOCK] = pick(row_blocks + b)
        return 0

    lax.fori_loop(0, row_blocks, regular, 0, unroll=8)

    def lead(k, _):
        for s in range(LEAD_SLOTS):
            lead_tiles_out[k, :, s * BLOCK : (s + 1) * BLOCK] = pick(
                2 * row_blocks + s * LEADS + k
            )
        at = pl.multiple_of(index_s[2, k] * BLOCK, BLOCK)
        lead_rows_out[k] = row_ref[:, pl.ds(at, BLOCK)]
        return 0

    lax.fori_loop(0, LEADS, lead, 0, unroll=2)


def kernel(
    n_z,
    n_camp,
    row_ref,
    tile_ref,
    lead_tile_ref,
    lead_row_ref,
    price_ref,
    spend_ref,
    step_ref,
    idx_ref,
    out_price,
    out_norm,
    rowaug,
    leadrow,
    colaug,
    leadaug,
    sel,
    selt,
    bias,
    pg,
    pgl,
    e_ref,
    el_ref,
    m_ref,
    l_ref,
    lse_ref,
    row_in,
    norm_in,
    norm_out,
    parts,
    cols,
    sib_in,
    z_out,
    z_in,
    prices,
    row_send,
    row_recv,
    norm_send,
    norm_recv,
    sib_send,
    sib_recv,
    z_send,
    z_recv,
    pz_send,
    pz_recv,
    pc_send,
    pc_recv,
):
    dp = lax.axis_index("dp")
    camp = lax.axis_index("camp")
    z = lax.div(dp, 2)
    core = lax.rem(dp, 2)
    sibling = 2 * z + 1 - core
    row_blocks = rowaug.shape[0]
    col_blocks = price_ref.shape[0]
    half = col_blocks // 2
    chunk = half // n_z
    band = BLOCK // n_camp

    barrier = pltpu.get_barrier_semaphore()

    def greet_camp(k, _):
        peer = lax.rem(camp + k, n_camp)
        pl.semaphore_signal(barrier, inc=1, device_id=(dp, peer), device_id_type=MESH)
        return 0

    lax.fori_loop(1, n_camp, greet_camp, 0)

    def greet_z(k, _):
        peer = lax.rem(z + k, n_z)
        pl.semaphore_signal(
            barrier, inc=1, device_id=(2 * peer + core, camp), device_id_type=MESH
        )
        return 0

    lax.fori_loop(1, n_z, greet_z, 0)
    pl.semaphore_signal(barrier, inc=1, device_id=(sibling, camp), device_id_type=MESH)

    block_id = idx_ref[0:1, :]
    valid = idx_ref[1:2, :]
    wide = block_id.shape[1]
    sel[...] = jnp.where(
        (lax.broadcasted_iota(jnp.int32, (col_blocks, wide), 0) == block_id) & (valid > 0),
        1.0,
        0.0,
    ).astype(BF16)
    both = jnp.concatenate(
        [block_id.astype(F32), valid.astype(F32), jnp.zeros((6, wide), F32)], axis=0
    )
    for half_t in range(2):
        part = both[:, half_t * BLOCK : (half_t + 1) * BLOCK]
        turned = jnp.concatenate([part, jnp.zeros((BLOCK - 8, BLOCK), F32)], axis=0).T
        at = turned[:, 0:1]
        ok = turned[:, 1:2]
        lanes = lax.broadcasted_iota(jnp.int32, (BLOCK, col_blocks), 1).astype(F32)
        selt[half_t * BLOCK : (half_t + 1) * BLOCK, :] = jnp.where(
            (lanes == at) & (ok > 0.5), 1.0, 0.0
        ).astype(BF16)
        bias[half_t * BLOCK : (half_t + 1) * BLOCK, :] = jnp.broadcast_to(
            jnp.where(ok > 0.5, 0.0, DEAD), (BLOCK, BLOCK)
        )

    def widen(tile):
        scaled = tile.astype(F32) * SCALE
        hi = scaled.astype(BF16).astype(F32)
        rest = scaled - hi
        mid = rest.astype(BF16).astype(F32)
        low = rest - mid
        stack = jnp.concatenate([hi, mid, low, jnp.zeros((RANK, BLOCK), F32)], axis=0)
        return stack.T.astype(BF16)

    def make_rows(b, _):
        at = pl.multiple_of(b * BLOCK, BLOCK)
        rowaug[b] = widen(row_ref[:, pl.ds(at, BLOCK)])
        return 0

    lax.fori_loop(0, row_blocks, make_rows, 0, unroll=2)

    def thrice(tile):
        return jnp.concatenate([tile, tile, tile, jnp.zeros_like(tile)], axis=0)

    def make_cols(b, _):
        colaug[b] = thrice(tile_ref[b])
        return 0

    lax.fori_loop(0, row_blocks, make_cols, 0, unroll=4)

    def make_leads(k, _):
        leadaug[k] = thrice(lead_tile_ref[k])
        leadrow[k] = widen(lead_row_ref[k])
        return 0

    lax.fori_loop(0, LEADS, make_leads, 0)

    prices[0] = price_ref[...]
    m_ref[...] = jnp.zeros_like(m_ref)
    l_ref[...] = jnp.zeros_like(l_ref)
    parts[...] = jnp.zeros_like(parts)
    pl.semaphore_wait(barrier, (n_camp - 1) + (n_z - 1) + 1)

    lane = lax.broadcasted_iota(jnp.int32, (BLOCK, BLOCK), 1)

    def place_of(k):
        places = idx_ref[2:3, 0:BLOCK]
        at = lax.broadcasted_iota(jnp.int32, (1, BLOCK), 1) == LEADS * LEAD_SLOTS + k
        return jnp.sum(jnp.where(at, places, 0), axis=1, keepdims=True)

    def one_pass(p, _):
        scaled_price = prices[p] * SCALE
        picked = exact_pick(selt[...], scaled_price) + bias[...]
        pg[:, 0:BLOCK] = picked[0:row_blocks]
        pg[:, BLOCK : 2 * BLOCK] = picked[row_blocks : 2 * row_blocks]
        for s in range(LEAD_SLOTS):
            base = 2 * row_blocks + s * LEADS
            pgl[:, s * BLOCK : (s + 1) * BLOCK] = picked[base : base + LEADS]

        def visit(g, _):
            m_all = m_ref[...]
            l_all = l_ref[...]
            for u in range(GROUP):
                b = g * GROUP + u
                logit = mm(rowaug[b], colaug[b]) - pg[pl.ds(b, 1), :]
                top = jnp.maximum(logit[:, 0:BLOCK], logit[:, BLOCK:])
                m = jnp.maximum(jnp.max(top, axis=1, keepdims=True), 0.0)
                e = jnp.exp2(logit - m)
                e_ref[b] = e
                l = jnp.sum(e[:, 0:BLOCK] + e[:, BLOCK:], axis=1, keepdims=True)
                m_all = jnp.where(lane == b, m, m_all)
                l_all = jnp.where(lane == b, l, l_all)
            m_ref[...] = m_all
            l_ref[...] = l_all
            return 0

        lax.fori_loop(0, row_blocks // GROUP, visit, 0)

        def visit_lead(k, _):
            place = place_of(k)
            logit = mm(leadrow[k], leadaug[k]) - pgl[pl.ds(k, 1), :]
            top = logit[:, 0:BLOCK]
            for s in range(1, LEAD_SLOTS):
                top = jnp.maximum(top, logit[:, s * BLOCK : (s + 1) * BLOCK])
            m = jnp.maximum(jnp.max(top, axis=1, keepdims=True), 0.0)
            e = jnp.exp2(logit - m)
            el_ref[k] = e
            total = e[:, 0:BLOCK]
            for s in range(1, LEAD_SLOTS):
                total = total + e[:, s * BLOCK : (s + 1) * BLOCK]
            l = jnp.sum(total, axis=1, keepdims=True)
            m_ref[...] = jnp.where(lane == place, m, m_ref[...])
            l_ref[...] = jnp.where(lane == place, l, l_ref[...])
            return 0

        lax.fori_loop(0, LEADS, visit_lead, 0)

        lse_ref[p] = m_ref[...] + jnp.log2(jnp.maximum(l_ref[...], 1e-37))
        mine = pl.ds(pl.multiple_of(camp * band, band), band)

        def send_rows(k, _):
            peer = lax.rem(camp + k, n_camp)
            theirs = pl.ds(pl.multiple_of(peer * band, band), band)
            pltpu.make_async_remote_copy(
                src_ref=lse_ref.at[p, theirs],
                dst_ref=row_in.at[p, camp],
                send_sem=row_send.at[p, peer],
                recv_sem=row_recv.at[p, camp],
                device_id=(dp, peer),
                device_id_type=MESH,
            ).start()
            return 0

        lax.fori_loop(1, n_camp, send_rows, 0)
        row_in[p, camp] = lse_ref[p, mine, :]

        def wait_rows(k, _):
            peer = lax.rem(camp + k, n_camp)
            pltpu.make_async_remote_copy(
                src_ref=row_in.at[p, peer],
                dst_ref=row_in.at[p, peer],
                send_sem=row_send.at[p, peer],
                recv_sem=row_recv.at[p, peer],
                device_id=(dp, peer),
                device_id_type=MESH,
            ).wait_recv()
            return 0

        lax.fori_loop(1, n_camp, wait_rows, 0)
        every = row_in[p]
        top = jnp.maximum(jnp.max(every, axis=0), 0.0)
        total = jnp.exp2(-top) + jnp.sum(jnp.exp2(every - top[None]), axis=0)
        norm = top + jnp.log2(total)
        norm_out[p] = norm
        norm_in[p, mine, :] = norm

        def send_norm(k, _):
            peer = lax.rem(camp + k, n_camp)
            pltpu.make_async_remote_copy(
                src_ref=norm_out.at[p],
                dst_ref=norm_in.at[p, mine],
                send_sem=norm_send.at[p, peer],
                recv_sem=norm_recv.at[p, camp],
                device_id=(dp, peer),
                device_id_type=MESH,
            ).start()
            return 0

        lax.fori_loop(1, n_camp, send_norm, 0)

        def wait_norm(k, _):
            peer = lax.rem(camp + k, n_camp)
            theirs = pl.ds(pl.multiple_of(peer * band, band), band)
            pltpu.make_async_remote_copy(
                src_ref=norm_in.at[p, theirs],
                dst_ref=norm_in.at[p, theirs],
                send_sem=norm_send.at[p, peer],
                recv_sem=norm_recv.at[p, peer],
                device_id=(dp, peer),
                device_id_type=MESH,
            ).wait_recv()
            return 0

        lax.fori_loop(1, n_camp, wait_norm, 0)

        l_ref[...] = jnp.exp2(m_ref[...] - norm_in[p])

        def weigh(g, _):
            turned = pltpu.roll(l_ref[...], lax.rem(BLOCK - g * GROUP, BLOCK), 1)
            for u in range(GROUP):
                b = g * GROUP + u
                part = jnp.sum(e_ref[b] * turned[:, u : u + 1], axis=0, keepdims=True)
                parts[pl.ds(b, 1), :] = part[:, 0:BLOCK]
                parts[pl.ds(row_blocks + b, 1), :] = part[:, BLOCK:]
            return 0

        lax.fori_loop(0, row_blocks // GROUP, weigh, 0)

        def weigh_lead(k, _):
            place = place_of(k)
            w = jnp.sum(jnp.where(lane == place, l_ref[...], 0.0), axis=1, keepdims=True)
            part = jnp.sum(el_ref[k] * w, axis=0, keepdims=True)
            for s in range(LEAD_SLOTS):
                parts[pl.ds(2 * row_blocks + s * LEADS + k, 1), :] = part[
                    :, s * BLOCK : (s + 1) * BLOCK
                ]
            return 0

        lax.fori_loop(0, LEADS, weigh_lead, 0)

        cols[p] = exact_pick(sel[...], parts[...])

        def send_sib(k, _):
            peer = lax.rem(z + k, n_z)
            at = pl.multiple_of((1 - core) * half + peer * chunk, chunk)
            pltpu.make_async_remote_copy(
                src_ref=cols.at[p, pl.ds(at, chunk)],
                dst_ref=sib_in.at[p, peer],
                send_sem=sib_send.at[p, peer],
                recv_sem=sib_recv.at[p, peer],
                device_id=(sibling, camp),
                device_id_type=MESH,
            ).start()
            return 0

        lax.fori_loop(1, n_z + 1, send_sib, 0)

        def wait_sib(peer):
            pltpu.make_async_remote_copy(
                src_ref=sib_in.at[p, peer],
                dst_ref=sib_in.at[p, peer],
                send_sem=sib_send.at[p, peer],
                recv_sem=sib_recv.at[p, peer],
                device_id=(sibling, camp),
                device_id_type=MESH,
            ).wait_recv()
            at = pl.multiple_of(core * half + peer * chunk, chunk)
            return cols[p, pl.ds(at, chunk), :] + sib_in[p, peer]

        def send_z(k, _):
            peer = lax.rem(z + k, n_z)
            z_out[p, peer] = wait_sib(peer)
            pltpu.make_async_remote_copy(
                src_ref=z_out.at[p, peer],
                dst_ref=z_in.at[p, z],
                send_sem=z_send.at[p, peer],
                recv_sem=z_recv.at[p, z],
                device_id=(2 * peer + core, camp),
                device_id_type=MESH,
            ).start()
            return 0

        lax.fori_loop(1, n_z, send_z, 0)
        total = wait_sib(z)

        def wait_z(k, total):
            peer = lax.rem(z + k, n_z)
            pltpu.make_async_remote_copy(
                src_ref=z_in.at[p, peer],
                dst_ref=z_in.at[p, peer],
                send_sem=z_send.at[p, peer],
                recv_sem=z_recv.at[p, peer],
                device_id=(2 * peer + core, camp),
                device_id_type=MESH,
            ).wait_recv()
            return total + z_in[p, peer]

        total = lax.fori_loop(1, n_z, wait_z, total)
        here = pl.ds(pl.multiple_of(core * half + z * chunk, chunk), chunk)
        prices[p + 1, here, :] = jnp.maximum(
            prices[p, here, :] + step_ref[p] * (total - spend_ref[here, :]), 0.0
        )

        def send_price(k, _):
            peer = lax.rem(z + k, n_z)
            pltpu.make_async_remote_copy(
                src_ref=prices.at[p + 1, here],
                dst_ref=prices.at[p + 1, here],
                send_sem=pz_send.at[p, peer],
                recv_sem=pz_recv.at[p, z],
                device_id=(2 * peer + core, camp),
                device_id_type=MESH,
            ).start()
            return 0

        lax.fori_loop(1, n_z, send_price, 0)

        def pass_on(peer):
            at = pl.ds(pl.multiple_of(core * half + peer * chunk, chunk), chunk)
            pltpu.make_async_remote_copy(
                src_ref=prices.at[p + 1, at],
                dst_ref=prices.at[p + 1, at],
                send_sem=pc_send.at[p, peer],
                recv_sem=pc_recv.at[p, peer],
                device_id=(sibling, camp),
                device_id_type=MESH,
            ).start()

        pass_on(z)

        def forward(k, _):
            peer = lax.rem(z + k, n_z)
            at = pl.ds(pl.multiple_of(core * half + peer * chunk, chunk), chunk)
            pltpu.make_async_remote_copy(
                src_ref=prices.at[p + 1, at],
                dst_ref=prices.at[p + 1, at],
                send_sem=pz_send.at[p, peer],
                recv_sem=pz_recv.at[p, peer],
                device_id=(2 * peer + core, camp),
                device_id_type=MESH,
            ).wait_recv()
            pass_on(peer)
            return 0

        lax.fori_loop(1, n_z, forward, 0)

        def wait_price(peer, _):
            at = pl.ds(pl.multiple_of((1 - core) * half + peer * chunk, chunk), chunk)
            pltpu.make_async_remote_copy(
                src_ref=prices.at[p + 1, at],
                dst_ref=prices.at[p + 1, at],
                send_sem=pc_send.at[p, peer],
                recv_sem=pc_recv.at[p, peer],
                device_id=(sibling, camp),
                device_id_type=MESH,
            ).wait_recv()
            return 0

        lax.fori_loop(0, n_z, wait_price, 0)
        return 0

    lax.fori_loop(0, PASSES, one_pass, 0)
    out_price[...] = prices[PASSES]
    out_norm[...] = (norm_in[PASSES - 1] * LN2).T[0:row_blocks, :]

    def drain(p, _):
        def drain_camp(k, _):
            peer = lax.rem(camp + k, n_camp)
            for src, sem in ((row_in, row_send), (row_in, norm_send)):
                pltpu.make_async_remote_copy(
                    src_ref=src.at[p, peer],
                    dst_ref=src.at[p, peer],
                    send_sem=sem.at[p, peer],
                    recv_sem=row_recv.at[p, peer],
                    device_id=(dp, peer),
                    device_id_type=MESH,
                ).wait_send()
            return 0

        lax.fori_loop(1, n_camp, drain_camp, 0)

        def drain_chunk(sem, peer):
            pltpu.make_async_remote_copy(
                src_ref=z_in.at[p, peer],
                dst_ref=z_in.at[p, peer],
                send_sem=sem.at[p, peer],
                recv_sem=z_recv.at[p, peer],
                device_id=(sibling, camp),
                device_id_type=MESH,
            ).wait_send()

        def drain_z(k, _):
            peer = lax.rem(z + k, n_z)
            drain_chunk(z_send, peer)
            drain_chunk(pz_send, peer)
            return 0

        lax.fori_loop(1, n_z, drain_z, 0)

        def drain_sib(peer, _):
            drain_chunk(sib_send, peer)
            drain_chunk(pc_send, peer)
            return 0

        lax.fori_loop(0, n_z, drain_sib, 0)
        return 0

    lax.fori_loop(0, PASSES, drain, 0)


def local(
    n_dp, n_camp, row_factors, col_factors, prices, spend_target, step_sizes, eligible, counts
):
    row_blocks, slots = eligible.shape
    col_blocks = prices.shape[0] // BLOCK
    n_z = n_dp // 2
    band = BLOCK // n_camp
    chunk = col_blocks // 2 // n_z
    wide = 256
    dma = pltpu.SemaphoreType.DMA
    vmem = pltpu.VMEM
    spec = pl.BlockSpec(memory_space=pltpu.VMEM)
    rows_t = row_factors.T
    smem = pl.BlockSpec(memory_space=pltpu.SMEM)
    index, tiles, lead_tiles, lead_rows = pl.pallas_call(
        functools.partial(gather_kernel, col_blocks),
        out_shape=(
            jax.ShapeDtypeStruct((8, wide), jnp.int32),
            jax.ShapeDtypeStruct((row_blocks, RANK, 2 * BLOCK), BF16),
            jax.ShapeDtypeStruct((LEADS, RANK, LEAD_SLOTS * BLOCK), BF16),
            jax.ShapeDtypeStruct((LEADS, RANK, BLOCK), BF16),
        ),
        in_specs=[spec, spec, spec, pl.BlockSpec(memory_space=pl.ANY)],
        out_specs=(spec,) * 4,
        scratch_shapes=[
            vmem((RANK, col_blocks * BLOCK), BF16),
            pltpu.SMEM((8, wide), jnp.int32),
            dma((2,)),
        ],
        compiler_params=pltpu.CompilerParams(vmem_limit_bytes=24 * 1024 * 1024),
    )(eligible.T, counts.reshape(1, row_blocks), rows_t, col_factors.T)
    new_prices, norms = pl.pallas_call(
        functools.partial(kernel, n_z, n_camp),
        out_shape=(
            jax.ShapeDtypeStruct((col_blocks, BLOCK), F32),
            jax.ShapeDtypeStruct((row_blocks, BLOCK), F32),
        ),
        in_specs=[spec] * 6 + [smem, spec],
        out_specs=(spec, spec),
        scratch_shapes=[
            vmem((row_blocks, BLOCK, BLOCK), BF16),
            vmem((LEADS, BLOCK, BLOCK), BF16),
            vmem((row_blocks, BLOCK, 2 * BLOCK), BF16),
            vmem((LEADS, BLOCK, LEAD_SLOTS * BLOCK), BF16),
            vmem((col_blocks, wide), BF16),
            vmem((wide, col_blocks), BF16),
            vmem((wide, BLOCK), F32),
            vmem((row_blocks, 2 * BLOCK), F32),
            vmem((LEADS, LEAD_SLOTS * BLOCK), F32),
            vmem((row_blocks, BLOCK, 2 * BLOCK), F32),
            vmem((LEADS, BLOCK, LEAD_SLOTS * BLOCK), F32),
            vmem((BLOCK, BLOCK), F32),
            vmem((BLOCK, BLOCK), F32),
            vmem((PASSES, BLOCK, BLOCK), F32),
            vmem((PASSES, n_camp, band, BLOCK), F32),
            vmem((PASSES, BLOCK, BLOCK), F32),
            vmem((PASSES, band, BLOCK), F32),
            vmem((wide, BLOCK), F32),
            vmem((PASSES, col_blocks, BLOCK), F32),
            vmem((PASSES, n_z, chunk, BLOCK), F32),
            vmem((PASSES, n_z, chunk, BLOCK), F32),
            vmem((PASSES, n_z, chunk, BLOCK), F32),
            vmem((PASSES + 1, col_blocks, BLOCK), F32),
            dma((PASSES, n_camp)),
            dma((PASSES, n_camp)),
            dma((PASSES, n_camp)),
            dma((PASSES, n_camp)),
            dma((PASSES, n_z)),
            dma((PASSES, n_z)),
            dma((PASSES, n_z)),
            dma((PASSES, n_z)),
            dma((PASSES, n_z)),
            dma((PASSES, n_z)),
            dma((PASSES, n_z)),
            dma((PASSES, n_z)),
        ],
        compiler_params=pltpu.CompilerParams(
            collective_id=0, has_side_effects=True, vmem_limit_bytes=40 * 1024 * 1024
        ),
    )(
        rows_t,
        tiles,
        lead_tiles,
        lead_rows,
        prices.reshape(col_blocks, BLOCK),
        spend_target.reshape(col_blocks, BLOCK),
        step_sizes,
        index,
    )
    return new_prices.reshape(-1), norms.reshape(-1)


def solution(mesh):
    placed = (P("dp", None), P("camp", None), P("camp"), P("camp"), P(), P("dp", None), P("dp"))
    return jax.shard_map(
        functools.partial(local, mesh.shape["dp"], mesh.shape["camp"]),
        mesh=mesh,
        in_specs=placed,
        out_specs=(P("camp"), P("dp")),
        check_vma=False,
    )
```

```python
import functools
import math

import jax
import jax.numpy as jnp
from jax import lax
from jax.experimental import pallas as pl
from jax.experimental.pallas import tpu as pltpu
from jax.sharding import PartitionSpec as P

MESH = pl.DeviceIdType.MESH
F32 = jnp.float32
BF16 = jnp.bfloat16
BLOCK = 128
RANK = 32
PASSES = 3
LEADS = 8
LEAD_SLOTS = 8
SCALE = math.log2(math.e) / 0.3
LN2 = math.log(2.0)
DEAD = 1e30
CHUNK = 16


def pieces(x):
    hi = x.astype(BF16)
    rest = x - hi.astype(F32)
    mid = rest.astype(BF16)
    low = (rest - mid.astype(F32)).astype(BF16)
    return hi, mid, low


def mm(a, b):
    return lax.dot_general(a, b, (((1,), (0,)), ((), ())), preferred_element_type=F32)


def mm_tn(a, b):
    return lax.dot_general(a, b, (((0,), (0,)), ((), ())), preferred_element_type=F32)


def mm_nt(a, b):
    return lax.dot_general(a, b, (((1,), (1,)), ((), ())), preferred_element_type=F32)


def exact_pick(select, x):
    hi, mid, low = pieces(x)
    out = mm(select, jnp.concatenate([hi, mid, low], axis=1))
    return out[:, :BLOCK] + out[:, BLOCK : 2 * BLOCK] + out[:, 2 * BLOCK :]


def slot_index(elig, cnt, own, col_blocks):
    slots, rows = elig.shape
    pos = lax.broadcasted_iota(jnp.int32, elig.shape, 0)
    owned = lax.div(elig, col_blocks) == own
    led = owned[0:1, :]
    first = jnp.min(jnp.where(owned, pos, slots), axis=0, keepdims=True)
    blocks, valids = [], []
    for k in range(2):
        picked = first + k
        chosen = jnp.sum(jnp.where(pos == picked, elig, 0), axis=0, keepdims=True)
        ok = (
            (picked < slots)
            & (lax.div(chosen, col_blocks) == own)
            & (picked < cnt)
            & jnp.logical_not(led)
        )
        blocks.append(jnp.where(ok, chosen - own * col_blocks, 0))
        valids.append(ok.astype(jnp.int32))
    led_f = jnp.broadcast_to(led.astype(F32), (8, rows))
    before = (
        lax.broadcasted_iota(jnp.int32, (rows, rows), 0)
        < lax.broadcasted_iota(jnp.int32, (rows, rows), 1)
    ).astype(F32)
    rank = mm(led_f.astype(BF16), before.astype(BF16))[0:1, :]
    lane = lax.broadcasted_iota(jnp.int32, (LEADS * LEAD_SLOTS, rows), 0)
    hot = jnp.where((rank == lax.rem(lane, LEADS).astype(F32)) & led, 1.0, 0.0)
    row_id = lax.broadcasted_iota(jnp.int32, (8, rows), 1).astype(F32)
    high = lax.div(elig, 128)
    picked = mm_nt(
        jnp.concatenate(
            [
                high.astype(F32),
                (elig - high * 128).astype(F32),
                jnp.broadcast_to(cnt, (8, rows)).astype(F32),
                jnp.ones((8, rows), F32),
                row_id,
            ],
            axis=0,
        ).astype(BF16),
        hot.astype(BF16),
    )
    wide = LEADS * LEAD_SLOTS
    every = picked[0:slots] * 128.0 + picked[slots : 2 * slots]
    slot_of = lax.div(lax.broadcasted_iota(jnp.int32, (slots, wide), 1), LEADS)
    chosen = jnp.sum(
        jnp.where(lax.broadcasted_iota(jnp.int32, (slots, wide), 0) == slot_of, every, 0.0),
        axis=0,
        keepdims=True,
    ).astype(jnp.int32)
    lead_cnt = picked[2 * slots : 2 * slots + 1]
    exists = picked[2 * slots + 8 : 2 * slots + 9] > 0.5
    lead_row = picked[2 * slots + 16 : 2 * slots + 17].astype(jnp.int32)
    ok = exists & (slot_of[0:1].astype(F32) < lead_cnt)
    blocks.append(jnp.where(ok, chosen - own * col_blocks, 0))
    valids.append(ok.astype(jnp.int32))
    blocks.append(jnp.zeros_like(lead_row))
    valids.append(jnp.zeros_like(lead_row))
    place = jnp.where(exists, lead_row, -1)
    return (
        jnp.concatenate(blocks, axis=1),
        jnp.concatenate(valids, axis=1),
        jnp.concatenate([lead_row, place, lead_row, place], axis=1),
    )


def gather_kernel(
    col_blocks,
    elig_hbm,
    cnt_hbm,
    row_hbm,
    col_hbm,
    index_out,
    tiles_out,
    lead_tiles_out,
    lead_rows_out,
    elig_ref,
    cnt_ref,
    row_ref,
    col_ref,
    index_s,
    sem,
):
    loads = [
        pltpu.make_async_copy(src, dst, sem.at[i])
        for i, (src, dst) in enumerate(
            ((elig_hbm, elig_ref), (cnt_hbm, cnt_ref), (col_hbm, col_ref), (row_hbm, row_ref))
        )
    ]
    for load in loads:
        load.start()
    own = lax.axis_index("camp")
    loads[0].wait()
    loads[1].wait()
    block_id, valid, lead_info = slot_index(elig_ref[...], cnt_ref[...], own, col_blocks)
    rest = jnp.zeros((5, block_id.shape[1]), jnp.int32)
    index_out[...] = jnp.concatenate([block_id, valid, lead_info, rest], axis=0)
    to_smem = pltpu.make_async_copy(index_out, index_s, sem.at[4])
    to_smem.start()
    to_smem.wait()
    loads[2].wait()
    row_blocks = tiles_out.shape[0]

    def pick(t):
        return col_ref[:, pl.ds(pl.multiple_of(index_s[0, t] * BLOCK, BLOCK), BLOCK)]

    def regular(b, _):
        tiles_out[b, :, 0:BLOCK] = pick(b)
        tiles_out[b, :, BLOCK : 2 * BLOCK] = pick(row_blocks + b)
        return 0

    lax.fori_loop(0, row_blocks, regular, 0, unroll=8)
    loads[3].wait()

    def lead(k, _):
        for s in range(LEAD_SLOTS):
            lead_tiles_out[k, :, s * BLOCK : (s + 1) * BLOCK] = pick(
                2 * row_blocks + s * LEADS + k
            )
        at = pl.multiple_of(index_s[2, k] * BLOCK, BLOCK)
        lead_rows_out[k] = row_ref[:, pl.ds(at, BLOCK)]
        return 0

    lax.fori_loop(0, LEADS, lead, 0, unroll=2)


def far_first(side):
    return sorted(range(1, side), key=lambda k: -min(k, side - k))


def kernel(
    n_z,
    side,
    row_hbm,
    tile_hbm,
    lead_tile_hbm,
    lead_row_hbm,
    price_hbm,
    spend_hbm,
    step_ref,
    idx_hbm,
    out_price,
    out_norm,
    row_ref,
    tile_ref,
    lead_tile_ref,
    lead_row_ref,
    spend_ref,
    idx_ref,
    sel,
    selt,
    bias,
    pg,
    pgl,
    s_ref,
    sl_ref,
    e_ref,
    el_ref,
    sum_ref,
    lead_sum_ref,
    m_ref,
    l_ref,
    ml_ref,
    ll_ref,
    turn_ref,
    lse_ref,
    row_in,
    parts,
    cols,
    sib_in,
    z_out,
    z_in,
    prices,
    load_sem,
    row_send,
    row_recv,
    sib_send,
    sib_recv,
    z_send,
    z_recv,
    pz_send,
    pz_recv,
    pc_send,
    pc_recv,
):
    dp = lax.axis_index("dp")
    camp = lax.axis_index("camp")
    z = lax.div(dp, 2)
    core = lax.rem(dp, 2)
    x = lax.div(camp, side)
    y = lax.rem(camp, side)
    sibling = 2 * z + 1 - core
    row_blocks = s_ref.shape[0]
    chunks = row_blocks // CHUNK
    col_blocks = spend_ref.shape[0]
    half = col_blocks // 2
    chunk = half // n_z
    n_camp = side * side

    loads = [
        pltpu.make_async_copy(src, dst, load_sem.at[i])
        for i, (src, dst) in enumerate(
            (
                (idx_hbm, idx_ref),
                (price_hbm, prices.at[0]),
                (row_hbm, row_ref),
                (tile_hbm, tile_ref),
                (lead_row_hbm, lead_row_ref),
                (lead_tile_hbm, lead_tile_ref),
                (spend_hbm, spend_ref),
            )
        )
    ]
    for load in loads:
        load.start()

    hops = [min(k, side - k) for k in range(side)]
    camp_peers = [
        lax.rem(x + dx, side) * side + lax.rem(y + dy, side)
        for dx, dy in sorted(
            ((a, b) for a in range(side) for b in range(side) if a or b),
            key=lambda ab: -hops[ab[0]] - hops[ab[1]],
        )
    ]
    z_peers = [lax.rem(z + k, n_z) for k in far_first(n_z)]

    barrier = pltpu.get_barrier_semaphore()
    for peer in camp_peers:
        pl.semaphore_signal(barrier, inc=1, device_id=(dp, peer), device_id_type=MESH)
    for peer in z_peers:
        pl.semaphore_signal(
            barrier, inc=1, device_id=(2 * peer + core, camp), device_id_type=MESH
        )
    pl.semaphore_signal(barrier, inc=1, device_id=(sibling, camp), device_id_type=MESH)

    loads[0].wait()
    block_id = idx_ref[0:1, :]
    valid = idx_ref[1:2, :]
    wide = block_id.shape[1]
    both = jnp.concatenate(
        [block_id.astype(F32), valid.astype(F32), jnp.zeros((6, wide), F32)], axis=0
    )
    for half_t in range(2):
        part = both[:, half_t * BLOCK : (half_t + 1) * BLOCK]
        turned = jnp.concatenate([part, jnp.zeros((BLOCK - 8, BLOCK), F32)], axis=0).T
        at = turned[:, 0:1]
        ok = turned[:, 1:2]
        lanes = lax.broadcasted_iota(jnp.int32, (BLOCK, col_blocks), 1).astype(F32)
        selt[half_t * BLOCK : (half_t + 1) * BLOCK, :] = jnp.where(
            (lanes == at) & (ok > 0.5), 1.0, 0.0
        ).astype(BF16)
        bias[half_t * BLOCK : (half_t + 1) * BLOCK, :] = jnp.broadcast_to(
            jnp.where(ok > 0.5, 0.0, DEAD), (BLOCK, BLOCK)
        )

    loads[2].wait()
    loads[3].wait()

    def score(b, _):
        at = pl.multiple_of(b * BLOCK, BLOCK)
        s_ref[b] = mm_tn(row_ref[:, pl.ds(at, BLOCK)], tile_ref[b]) * SCALE
        return 0

    lax.fori_loop(0, row_blocks, score, 0, unroll=8)
    loads[4].wait()
    loads[5].wait()

    def score_lead(k, _):
        sl_ref[k] = mm_tn(lead_row_ref[k], lead_tile_ref[k]) * SCALE
        return 0

    lax.fori_loop(0, LEADS, score_lead, 0, unroll=2)

    parts[...] = jnp.zeros_like(parts)
    turn_ref[...] = jnp.zeros_like(turn_ref)
    loads[1].wait()
    loads[6].wait()
    pl.semaphore_wait(barrier, (n_camp - 1) + (n_z - 1) + 1)

    lane = lax.broadcasted_iota(jnp.int32, (BLOCK, BLOCK), 1)

    def place_of(k):
        places = idx_ref[2:3, 0:BLOCK]
        at = lax.broadcasted_iota(jnp.int32, (1, BLOCK), 1) == LEADS * LEAD_SLOTS + k
        return jnp.sum(jnp.where(at, places, 0), axis=1, keepdims=True)

    def price_rows(of_core, peer):
        return pl.ds(pl.multiple_of(of_core * half + peer * chunk, chunk), chunk)

    def row_copy(p, c, src, dst, peer, slot):
        rows = pl.ds(pl.multiple_of(c * CHUNK, CHUNK), CHUNK)
        return pltpu.make_async_remote_copy(
            src_ref=src.at[p, rows],
            dst_ref=dst.at[p, slot, rows],
            send_sem=row_send.at[p, c, peer],
            recv_sem=row_recv.at[p, c, slot],
            device_id=(dp, peer),
            device_id_type=MESH,
        )

    def sib_copy(p, peer):
        return pltpu.make_async_remote_copy(
            src_ref=cols.at[p, price_rows(1 - core, peer)],
            dst_ref=sib_in.at[p, peer],
            send_sem=sib_send.at[p, peer],
            recv_sem=sib_recv.at[p, peer],
            device_id=(sibling, camp),
            device_id_type=MESH,
        )

    def z_copy(p, peer, slot):
        return pltpu.make_async_remote_copy(
            src_ref=z_out.at[p, peer],
            dst_ref=z_in.at[p, slot],
            send_sem=z_send.at[p, peer],
            recv_sem=z_recv.at[p, slot],
            device_id=(2 * peer + core, camp),
            device_id_type=MESH,
        )

    def price_copy(p, peer, owner):
        rows = price_rows(core, owner)
        return pltpu.make_async_remote_copy(
            src_ref=prices.at[p + 1, rows],
            dst_ref=prices.at[p + 1, rows],
            send_sem=pz_send.at[p, peer],
            recv_sem=pz_recv.at[p, owner],
            device_id=(2 * peer + core, camp),
            device_id_type=MESH,
        )

    def cross_copy(p, of_core, owner):
        rows = price_rows(of_core, owner)
        return pltpu.make_async_remote_copy(
            src_ref=prices.at[p + 1, rows],
            dst_ref=prices.at[p + 1, rows],
            send_sem=pc_send.at[p, owner],
            recv_sem=pc_recv.at[p, owner],
            device_id=(sibling, camp),
            device_id_type=MESH,
        )

    def one_pass(p, _):
        picked = exact_pick(selt[...], prices[p] * SCALE) + bias[...]
        pg[:, 0:BLOCK] = picked[0:row_blocks]
        pg[:, BLOCK : 2 * BLOCK] = picked[row_blocks : 2 * row_blocks]
        for s in range(LEAD_SLOTS):
            base = 2 * row_blocks + s * LEADS
            pgl[:, s * BLOCK : (s + 1) * BLOCK] = picked[base : base + LEADS]
        ml_ref[...] = jnp.zeros_like(ml_ref)
        ll_ref[...] = jnp.zeros_like(ll_ref)

        def visit_lead(k, _):
            place = place_of(k)
            price = pgl[pl.ds(k, 1), :]
            for r in range(0, BLOCK, 32):
                logit = sl_ref[k, r : r + 32, :] - price
                top = logit[:, 0:BLOCK]
                for s in range(1, LEAD_SLOTS):
                    top = jnp.maximum(top, logit[:, s * BLOCK : (s + 1) * BLOCK])
                m = jnp.maximum(jnp.max(top, axis=1, keepdims=True), 0.0)
                e = jnp.exp2(logit - m)
                el_ref[k, r : r + 32, :] = e
                total = e[:, 0:BLOCK]
                for s in range(1, LEAD_SLOTS):
                    total = total + e[:, s * BLOCK : (s + 1) * BLOCK]
                lead_sum_ref[k, r : r + 32, :] = total
                ml_ref[r : r + 32, :] = jnp.where(
                    lane[r : r + 32] == place, m, ml_ref[r : r + 32, :]
                )
            return 0

        lax.fori_loop(0, LEADS, visit_lead, 0, unroll=2)

        def add_lead(k, _):
            place = place_of(k)
            l = jnp.sum(lead_sum_ref[k], axis=1, keepdims=True)
            ll_ref[...] = jnp.where(lane == place, l, ll_ref[...])
            return 0

        lax.fori_loop(0, LEADS, add_lead, 0, unroll=8)
        m_ref[...] = ml_ref[...]

        def visit(c, _):
            m_all = jnp.zeros((BLOCK, BLOCK), F32)
            for u in range(CHUNK):
                b = c * CHUNK + u
                logit = s_ref[b] - pg[pl.ds(b, 1), :]
                top = jnp.maximum(logit[:, 0:BLOCK], logit[:, BLOCK:])
                m = jnp.maximum(jnp.max(top, axis=1, keepdims=True), 0.0)
                e = jnp.exp2(logit - m)
                e_ref[b] = e
                sum_ref[u] = e[:, 0:BLOCK] + e[:, BLOCK:]
                m_all = jnp.where(lane == b, m, m_all)
            m_ref[...] = m_ref[...] + m_all
            l_all = ll_ref[...]
            for u in range(CHUNK):
                l = jnp.sum(sum_ref[u], axis=1, keepdims=True)
                l_all = l_all + jnp.where(lane == c * CHUNK + u, l, 0.0)
            l_ref[...] = (m_ref[...] + jnp.log2(jnp.maximum(l_all, 1e-37))).T
            rows = pl.ds(pl.multiple_of(c * CHUNK, CHUNK), CHUNK)
            lse = l_ref[rows, :]
            lse_ref[p, rows, :] = lse
            row_in[p, camp, rows, :] = lse
            for peer in camp_peers:
                row_copy(p, c, lse_ref, row_in, peer, camp).start()
            return 0

        lax.fori_loop(0, chunks, visit, 0)

        @pl.when(p == 0)
        def _():
            sel[...] = jnp.where(
                (lax.broadcasted_iota(jnp.int32, (col_blocks, wide), 0) == block_id)
                & (valid > 0),
                1.0,
                0.0,
            ).astype(BF16)

        def weigh(c, _):
            rows = pl.ds(pl.multiple_of(c * CHUNK, CHUNK), CHUNK)
            for peer in camp_peers[::-1]:
                row_copy(p, c, lse_ref, row_in, peer, peer).wait_recv()
            every = row_in[p, :, rows, :]
            top = jnp.maximum(jnp.max(every, axis=0), 0.0)
            total = jnp.exp2(-top) + jnp.sum(jnp.exp2(every - top[None]), axis=0)
            turn_ref[rows, :] = top + jnp.log2(total)
            weight = jnp.exp2(m_ref[...] - turn_ref[...].T)
            l_ref[...] = weight
            turned = pltpu.roll(weight, lax.rem(BLOCK - c * CHUNK, BLOCK), 1)
            first, second = [], []
            for u in range(CHUNK):
                part = jnp.sum(
                    e_ref[c * CHUNK + u] * turned[:, u : u + 1], axis=0, keepdims=True
                )
                first.append(part[:, 0:BLOCK])
                second.append(part[:, BLOCK:])
            parts[rows, :] = jnp.concatenate(first, axis=0)
            parts[pl.ds(pl.multiple_of(row_blocks + c * CHUNK, CHUNK), CHUNK), :] = (
                jnp.concatenate(second, axis=0)
            )
            return 0

        lax.fori_loop(0, chunks, weigh, 0)

        def weigh_lead(k, _):
            place = place_of(k)
            w = jnp.sum(jnp.where(lane == place, l_ref[...], 0.0), axis=1, keepdims=True)
            part = jnp.sum(el_ref[k] * w, axis=0, keepdims=True)
            for s in range(LEAD_SLOTS):
                parts[pl.ds(2 * row_blocks + s * LEADS + k, 1), :] = part[
                    :, s * BLOCK : (s + 1) * BLOCK
                ]
            return 0

        lax.fori_loop(0, LEADS, weigh_lead, 0, unroll=4)

        cols[p] = exact_pick(sel[...], parts[...])
        for peer in z_peers:
            sib_copy(p, peer).start()
        sib_copy(p, z).start()
        for peer in z_peers:
            sib_copy(p, peer).wait_recv()
            z_out[p, peer] = cols[p, price_rows(core, peer), :] + sib_in[p, peer]
            z_copy(p, peer, z).start()
        sib_copy(p, z).wait_recv()
        here = price_rows(core, z)
        total = cols[p, here, :] + sib_in[p, z]
        for peer in z_peers[::-1]:
            z_copy(p, peer, peer).wait_recv()
            total = total + z_in[p, peer]
        prices[p + 1, here, :] = jnp.maximum(
            prices[p, here, :] + step_ref[p] * (total - spend_ref[here, :]), 0.0
        )
        for peer in z_peers:
            price_copy(p, peer, z).start()
        cross_copy(p, core, z).start()
        for peer in z_peers[::-1]:
            price_copy(p, peer, peer).wait_recv()
            cross_copy(p, core, peer).start()
        cross_copy(p, 1 - core, z).wait_recv()
        for peer in z_peers[::-1]:
            cross_copy(p, 1 - core, peer).wait_recv()
        return 0

    lax.fori_loop(0, PASSES, one_pass, 0)
    out_price[...] = prices[PASSES]
    out_norm[...] = turn_ref[0:row_blocks, :] * LN2

    def drain(p, _):
        def drain_rows(c, _):
            for peer in camp_peers:
                row_copy(p, c, lse_ref, row_in, peer, camp).wait_send()
            return 0

        lax.fori_loop(0, chunks, drain_rows, 0)
        for peer in z_peers:
            sib_copy(p, peer).wait_send()
            z_copy(p, peer, z).wait_send()
            price_copy(p, peer, z).wait_send()
            cross_copy(p, core, peer).wait_send()
        sib_copy(p, z).wait_send()
        cross_copy(p, core, z).wait_send()
        return 0

    lax.fori_loop(0, PASSES, drain, 0)


def local(
    n_dp, n_camp, row_factors, col_factors, prices, spend_target, step_sizes, eligible, counts
):
    row_blocks, slots = eligible.shape
    col_blocks = prices.shape[0] // BLOCK
    n_z = n_dp // 2
    side = math.isqrt(n_camp)
    chunk = col_blocks // 2 // n_z
    chunks = row_blocks // CHUNK
    wide = 256
    dma = pltpu.SemaphoreType.DMA
    vmem = pltpu.VMEM
    spec = pl.BlockSpec(memory_space=pltpu.VMEM)
    smem = pl.BlockSpec(memory_space=pltpu.SMEM)
    hbm = pl.BlockSpec(memory_space=pltpu.HBM)
    rows_t = row_factors.T
    index, tiles, lead_tiles, lead_rows = pl.pallas_call(
        functools.partial(gather_kernel, col_blocks),
        out_shape=(
            jax.ShapeDtypeStruct((8, wide), jnp.int32),
            jax.ShapeDtypeStruct((row_blocks, RANK, 2 * BLOCK), BF16),
            jax.ShapeDtypeStruct((LEADS, RANK, LEAD_SLOTS * BLOCK), BF16),
            jax.ShapeDtypeStruct((LEADS, RANK, BLOCK), BF16),
        ),
        in_specs=[hbm] * 4,
        out_specs=(spec,) * 4,
        scratch_shapes=[
            vmem((slots, row_blocks), jnp.int32),
            vmem((1, row_blocks), jnp.int32),
            vmem(rows_t.shape, BF16),
            vmem((RANK, col_blocks * BLOCK), BF16),
            pltpu.SMEM((8, wide), jnp.int32),
            dma((5,)),
        ],
        compiler_params=pltpu.CompilerParams(vmem_limit_bytes=60 * 1024 * 1024),
    )(eligible.T, counts.reshape(1, row_blocks), rows_t, col_factors.T)
    per_z = (PASSES, n_z, chunk, BLOCK)
    square = vmem((BLOCK, BLOCK), F32)
    new_prices, norms = pl.pallas_call(
        functools.partial(kernel, n_z, side),
        out_shape=(
            jax.ShapeDtypeStruct((col_blocks, BLOCK), F32),
            jax.ShapeDtypeStruct((row_blocks, BLOCK), F32),
        ),
        in_specs=[hbm] * 6 + [smem, hbm],
        out_specs=(spec, spec),
        scratch_shapes=[
            vmem(rows_t.shape, BF16),
            vmem(tiles.shape, BF16),
            vmem(lead_tiles.shape, BF16),
            vmem(lead_rows.shape, BF16),
            vmem((col_blocks, BLOCK), F32),
            vmem((8, wide), jnp.int32),
            vmem((col_blocks, wide), BF16),
            vmem((wide, col_blocks), BF16),
            vmem((wide, BLOCK), F32),
            vmem((row_blocks, 2 * BLOCK), F32),
            vmem((LEADS, LEAD_SLOTS * BLOCK), F32),
            vmem((row_blocks, BLOCK, 2 * BLOCK), F32),
            vmem((LEADS, BLOCK, LEAD_SLOTS * BLOCK), F32),
            vmem((row_blocks, BLOCK, 2 * BLOCK), F32),
            vmem((LEADS, BLOCK, LEAD_SLOTS * BLOCK), F32),
            vmem((CHUNK, BLOCK, BLOCK), F32),
            vmem((LEADS, BLOCK, BLOCK), F32),
            square,
            square,
            square,
            square,
            square,
            vmem((PASSES, row_blocks, BLOCK), F32),
            vmem((PASSES, n_camp, row_blocks, BLOCK), F32),
            vmem((wide, BLOCK), F32),
            vmem((PASSES, col_blocks, BLOCK), F32),
            vmem(per_z, F32),
            vmem(per_z, F32),
            vmem(per_z, F32),
            vmem((PASSES + 1, col_blocks, BLOCK), F32),
            dma((7,)),
            dma((PASSES, chunks, n_camp)),
            dma((PASSES, chunks, n_camp)),
        ]
        + [dma((PASSES, n_z))] * 8,
        compiler_params=pltpu.CompilerParams(
            collective_id=0, has_side_effects=True, vmem_limit_bytes=56 * 1024 * 1024
        ),
    )(
        rows_t,
        tiles,
        lead_tiles,
        lead_rows,
        prices.reshape(col_blocks, BLOCK),
        spend_target.reshape(col_blocks, BLOCK),
        step_sizes,
        index,
    )
    return new_prices.reshape(-1), norms.reshape(-1)


def solution(mesh):
    placed = (P("dp", None), P("camp", None), P("camp"), P("camp"), P(), P("dp", None), P("dp"))
    return jax.shard_map(
        functools.partial(local, mesh.shape["dp"], mesh.shape["camp"]),
        mesh=mesh,
        in_specs=placed,
        out_specs=(P("camp"), P("dp")),
        check_vma=False,
    )
```

```python
import functools
import math

import jax
import jax.numpy as jnp
from jax import lax
from jax.experimental import pallas as pl
from jax.experimental.pallas import tpu as pltpu
from jax.sharding import PartitionSpec as P

MESH = pl.DeviceIdType.MESH
F32 = jnp.float32
BF16 = jnp.bfloat16
BLOCK = 128
RANK = 32
PASSES = 3
LEADS = 8
LEAD_SLOTS = 8
SCALE = math.log2(math.e) / 0.3
LN2 = math.log(2.0)
DEAD = 1e30
CHUNK = 32


def pieces(x):
    hi = x.astype(BF16)
    rest = x - hi.astype(F32)
    mid = rest.astype(BF16)
    low = (rest - mid.astype(F32)).astype(BF16)
    return hi, mid, low


def mm(a, b):
    return lax.dot_general(a, b, (((1,), (0,)), ((), ())), preferred_element_type=F32)


def mm_tn(a, b):
    return lax.dot_general(a, b, (((0,), (0,)), ((), ())), preferred_element_type=F32)


def mm_nt(a, b):
    return lax.dot_general(a, b, (((1,), (1,)), ((), ())), preferred_element_type=F32)


def exact_pick(select, x):
    hi, mid, low = pieces(x)
    out = mm(select, jnp.concatenate([hi, mid, low], axis=1))
    return out[:, :BLOCK] + out[:, BLOCK : 2 * BLOCK] + out[:, 2 * BLOCK :]


def slot_index(elig, cnt, own, col_blocks):
    slots, rows = elig.shape
    pos = lax.broadcasted_iota(jnp.int32, elig.shape, 0)
    owned = lax.div(elig, col_blocks) == own
    led = owned[0:1, :]
    first = jnp.min(jnp.where(owned, pos, slots), axis=0, keepdims=True)
    blocks, valids = [], []
    for k in range(2):
        picked = first + k
        chosen = jnp.sum(jnp.where(pos == picked, elig, 0), axis=0, keepdims=True)
        ok = (
            (picked < slots)
            & (lax.div(chosen, col_blocks) == own)
            & (picked < cnt)
            & jnp.logical_not(led)
        )
        blocks.append(jnp.where(ok, chosen - own * col_blocks, 0))
        valids.append(ok.astype(jnp.int32))
    led_f = jnp.broadcast_to(led.astype(F32), (8, rows))
    before = (
        lax.broadcasted_iota(jnp.int32, (rows, rows), 0)
        < lax.broadcasted_iota(jnp.int32, (rows, rows), 1)
    ).astype(F32)
    rank = mm(led_f.astype(BF16), before.astype(BF16))[0:1, :]
    lane = lax.broadcasted_iota(jnp.int32, (LEADS * LEAD_SLOTS, rows), 0)
    hot = jnp.where((rank == lax.rem(lane, LEADS).astype(F32)) & led, 1.0, 0.0)
    row_id = lax.broadcasted_iota(jnp.int32, (8, rows), 1).astype(F32)
    high = lax.div(elig, 128)
    picked = mm_nt(
        jnp.concatenate(
            [
                high.astype(F32),
                (elig - high * 128).astype(F32),
                jnp.broadcast_to(cnt, (8, rows)).astype(F32),
                jnp.ones((8, rows), F32),
                row_id,
            ],
            axis=0,
        ).astype(BF16),
        hot.astype(BF16),
    )
    wide = LEADS * LEAD_SLOTS
    every = picked[0:slots] * 128.0 + picked[slots : 2 * slots]
    slot_of = lax.div(lax.broadcasted_iota(jnp.int32, (slots, wide), 1), LEADS)
    chosen = jnp.sum(
        jnp.where(lax.broadcasted_iota(jnp.int32, (slots, wide), 0) == slot_of, every, 0.0),
        axis=0,
        keepdims=True,
    ).astype(jnp.int32)
    lead_cnt = picked[2 * slots : 2 * slots + 1]
    exists = picked[2 * slots + 8 : 2 * slots + 9] > 0.5
    lead_row = picked[2 * slots + 16 : 2 * slots + 17].astype(jnp.int32)
    ok = exists & (slot_of[0:1].astype(F32) < lead_cnt)
    blocks.append(jnp.where(ok, chosen - own * col_blocks, 0))
    valids.append(ok.astype(jnp.int32))
    blocks.append(jnp.zeros_like(lead_row))
    valids.append(jnp.zeros_like(lead_row))
    place = jnp.where(exists, lead_row, -1)
    return (
        jnp.concatenate(blocks, axis=1),
        jnp.concatenate(valids, axis=1),
        jnp.concatenate([lead_row, place, lead_row, place], axis=1),
    )


def gather_kernel(
    col_blocks,
    elig_hbm,
    cnt_hbm,
    row_hbm,
    col_hbm,
    index_out,
    tiles_out,
    lead_tiles_out,
    lead_rows_out,
    elig_ref,
    cnt_ref,
    row_ref,
    col_ref,
    index_s,
    sem,
):
    loads = [
        pltpu.make_async_copy(src, dst, sem.at[i])
        for i, (src, dst) in enumerate(
            ((elig_hbm, elig_ref), (cnt_hbm, cnt_ref), (col_hbm, col_ref), (row_hbm, row_ref))
        )
    ]
    for load in loads:
        load.start()
    own = lax.axis_index("camp")
    loads[0].wait()
    loads[1].wait()
    block_id, valid, lead_info = slot_index(elig_ref[...], cnt_ref[...], own, col_blocks)
    rest = jnp.zeros((5, block_id.shape[1]), jnp.int32)
    index_out[...] = jnp.concatenate([block_id, valid, lead_info, rest], axis=0)
    to_smem = pltpu.make_async_copy(index_out, index_s, sem.at[4])
    to_smem.start()
    to_smem.wait()
    loads[2].wait()
    row_blocks = tiles_out.shape[0]

    def pick(t):
        return col_ref[:, pl.ds(pl.multiple_of(index_s[0, t] * BLOCK, BLOCK), BLOCK)]

    def regular(b, _):
        tiles_out[b, :, 0:BLOCK] = pick(b)
        tiles_out[b, :, BLOCK : 2 * BLOCK] = pick(row_blocks + b)
        return 0

    lax.fori_loop(0, row_blocks, regular, 0, unroll=8)
    loads[3].wait()

    def lead(k, _):
        for s in range(LEAD_SLOTS):
            lead_tiles_out[k, :, s * BLOCK : (s + 1) * BLOCK] = pick(
                2 * row_blocks + s * LEADS + k
            )
        at = pl.multiple_of(index_s[2, k] * BLOCK, BLOCK)
        lead_rows_out[k] = row_ref[:, pl.ds(at, BLOCK)]
        return 0

    lax.fori_loop(0, LEADS, lead, 0, unroll=2)


def far_first(side):
    return sorted(range(1, side), key=lambda k: -min(k, side - k))


def kernel(
    n_z,
    side,
    row_ref,
    tile_ref,
    lead_tile_ref,
    lead_row_ref,
    price_ref,
    spend_ref,
    step_ref,
    idx_ref,
    out_price,
    out_norm,
    sel,
    selt,
    bias,
    pg,
    pgl,
    s_ref,
    sl_ref,
    e_ref,
    el_ref,
    sum_ref,
    lead_sum_ref,
    m_ref,
    l_ref,
    ml_ref,
    ll_ref,
    turn_ref,
    lse_ref,
    row_in,
    parts,
    cols,
    sib_in,
    z_out,
    z_in,
    prices,
    row_send,
    row_recv,
    sib_send,
    sib_recv,
    z_send,
    z_recv,
    pz_send,
    pz_recv,
    pc_send,
    pc_recv,
):
    dp = lax.axis_index("dp")
    camp = lax.axis_index("camp")
    z = lax.div(dp, 2)
    core = lax.rem(dp, 2)
    x = lax.div(camp, side)
    y = lax.rem(camp, side)
    sibling = 2 * z + 1 - core
    row_blocks = s_ref.shape[0]
    chunks = row_blocks // CHUNK
    col_blocks = spend_ref.shape[0]
    half = col_blocks // 2
    chunk = half // n_z
    n_camp = side * side

    hops = [min(k, side - k) for k in range(side)]
    camp_peers = [
        lax.rem(x + dx, side) * side + lax.rem(y + dy, side)
        for dx, dy in sorted(
            ((a, b) for a in range(side) for b in range(side) if a or b),
            key=lambda ab: -hops[ab[0]] - hops[ab[1]],
        )
    ]
    z_peers = [lax.rem(z + k, n_z) for k in far_first(n_z)]

    barrier = pltpu.get_barrier_semaphore()
    for peer in camp_peers:
        pl.semaphore_signal(barrier, inc=1, device_id=(dp, peer), device_id_type=MESH)
    for peer in z_peers:
        pl.semaphore_signal(
            barrier, inc=1, device_id=(2 * peer + core, camp), device_id_type=MESH
        )
    pl.semaphore_signal(barrier, inc=1, device_id=(sibling, camp), device_id_type=MESH)

    block_id = idx_ref[0:1, :]
    valid = idx_ref[1:2, :]
    wide = block_id.shape[1]
    both = jnp.concatenate(
        [block_id.astype(F32), valid.astype(F32), jnp.zeros((6, wide), F32)], axis=0
    )
    for half_t in range(2):
        part = both[:, half_t * BLOCK : (half_t + 1) * BLOCK]
        turned = jnp.concatenate([part, jnp.zeros((BLOCK - 8, BLOCK), F32)], axis=0).T
        at = turned[:, 0:1]
        ok = turned[:, 1:2]
        lanes = lax.broadcasted_iota(jnp.int32, (BLOCK, col_blocks), 1).astype(F32)
        selt[half_t * BLOCK : (half_t + 1) * BLOCK, :] = jnp.where(
            (lanes == at) & (ok > 0.5), 1.0, 0.0
        ).astype(BF16)
        bias[half_t * BLOCK : (half_t + 1) * BLOCK, :] = jnp.broadcast_to(
            jnp.where(ok > 0.5, 0.0, DEAD), (BLOCK, BLOCK)
        )

    def score(b, _):
        at = pl.multiple_of(b * BLOCK, BLOCK)
        s_ref[b] = mm_tn(row_ref[:, pl.ds(at, BLOCK)], tile_ref[b]) * SCALE
        return 0

    lax.fori_loop(0, row_blocks, score, 0, unroll=32)

    def score_lead(k, _):
        sl_ref[k] = mm_tn(lead_row_ref[k], lead_tile_ref[k]) * SCALE
        return 0

    lax.fori_loop(0, LEADS, score_lead, 0, unroll=8)

    parts[...] = jnp.zeros_like(parts)
    turn_ref[...] = jnp.zeros_like(turn_ref)
    prices[0] = price_ref[...]

    lane = lax.broadcasted_iota(jnp.int32, (BLOCK, BLOCK), 1)

    def place_of(k):
        places = idx_ref[2:3, 0:BLOCK]
        at = lax.broadcasted_iota(jnp.int32, (1, BLOCK), 1) == LEADS * LEAD_SLOTS + k
        return jnp.sum(jnp.where(at, places, 0), axis=1, keepdims=True)

    def price_rows(of_core, peer):
        return pl.ds(pl.multiple_of(of_core * half + peer * chunk, chunk), chunk)

    def row_copy(p, c, src, dst, peer, slot):
        rows = pl.ds(pl.multiple_of(c * CHUNK, CHUNK), CHUNK)
        return pltpu.make_async_remote_copy(
            src_ref=src.at[p, rows],
            dst_ref=dst.at[p, slot, rows],
            send_sem=row_send.at[p, c, peer],
            recv_sem=row_recv.at[p, c, slot],
            device_id=(dp, peer),
            device_id_type=MESH,
        )

    def sib_copy(p, peer):
        return pltpu.make_async_remote_copy(
            src_ref=cols.at[p, price_rows(1 - core, peer)],
            dst_ref=sib_in.at[p, peer],
            send_sem=sib_send.at[p, peer],
            recv_sem=sib_recv.at[p, peer],
            device_id=(sibling, camp),
            device_id_type=MESH,
        )

    def z_copy(p, peer, slot):
        return pltpu.make_async_remote_copy(
            src_ref=z_out.at[p, peer],
            dst_ref=z_in.at[p, slot],
            send_sem=z_send.at[p, peer],
            recv_sem=z_recv.at[p, slot],
            device_id=(2 * peer + core, camp),
            device_id_type=MESH,
        )

    def price_copy(p, peer, owner):
        rows = price_rows(core, owner)
        return pltpu.make_async_remote_copy(
            src_ref=prices.at[p + 1, rows],
            dst_ref=prices.at[p + 1, rows],
            send_sem=pz_send.at[p, peer],
            recv_sem=pz_recv.at[p, owner],
            device_id=(2 * peer + core, camp),
            device_id_type=MESH,
        )

    def cross_copy(p, of_core, owner):
        rows = price_rows(of_core, owner)
        return pltpu.make_async_remote_copy(
            src_ref=prices.at[p + 1, rows],
            dst_ref=prices.at[p + 1, rows],
            send_sem=pc_send.at[p, owner],
            recv_sem=pc_recv.at[p, owner],
            device_id=(sibling, camp),
            device_id_type=MESH,
        )

    def one_pass(p, _):
        picked = exact_pick(selt[...], prices[p] * SCALE) + bias[...]
        pg[:, 0:BLOCK] = picked[0:row_blocks]
        pg[:, BLOCK : 2 * BLOCK] = picked[row_blocks : 2 * row_blocks]
        for s in range(LEAD_SLOTS):
            base = 2 * row_blocks + s * LEADS
            pgl[:, s * BLOCK : (s + 1) * BLOCK] = picked[base : base + LEADS]
        ml_ref[...] = jnp.zeros_like(ml_ref)
        ll_ref[...] = jnp.zeros_like(ll_ref)

        def visit_lead(k, _):
            place = place_of(k)
            price = pgl[pl.ds(k, 1), :]
            for r in range(0, BLOCK, 32):
                logit = sl_ref[k, r : r + 32, :] - price
                top = logit[:, 0:BLOCK]
                for s in range(1, LEAD_SLOTS):
                    top = jnp.maximum(top, logit[:, s * BLOCK : (s + 1) * BLOCK])
                m = jnp.maximum(jnp.max(top, axis=1, keepdims=True), 0.0)
                e = jnp.exp2(logit - m)
                el_ref[k, r : r + 32, :] = e
                total = e[:, 0:BLOCK]
                for s in range(1, LEAD_SLOTS):
                    total = total + e[:, s * BLOCK : (s + 1) * BLOCK]
                lead_sum_ref[k, r : r + 32, :] = total
                ml_ref[r : r + 32, :] = jnp.where(
                    lane[r : r + 32] == place, m, ml_ref[r : r + 32, :]
                )
            return 0

        lax.fori_loop(0, LEADS, visit_lead, 0, unroll=2)

        def add_lead(k, _):
            place = place_of(k)
            l = jnp.sum(lead_sum_ref[k], axis=1, keepdims=True)
            ll_ref[...] = jnp.where(lane == place, l, ll_ref[...])
            return 0

        lax.fori_loop(0, LEADS, add_lead, 0, unroll=8)
        m_ref[...] = ml_ref[...]

        def visit(c, _):
            m_all = jnp.zeros((BLOCK, BLOCK), F32)
            for u in range(CHUNK):
                b = c * CHUNK + u
                logit = s_ref[b] - pg[pl.ds(b, 1), :]
                top = jnp.maximum(logit[:, 0:BLOCK], logit[:, BLOCK:])
                m = jnp.maximum(jnp.max(top, axis=1, keepdims=True), 0.0)
                e = jnp.exp2(logit - m)
                e_ref[b] = e
                sum_ref[u] = e[:, 0:BLOCK] + e[:, BLOCK:]
                m_all = jnp.where(lane == b, m, m_all)
            m_ref[...] = m_ref[...] + m_all
            l_all = ll_ref[...]
            for u in range(CHUNK):
                l = jnp.sum(sum_ref[u], axis=1, keepdims=True)
                l_all = l_all + jnp.where(lane == c * CHUNK + u, l, 0.0)
            l_ref[...] = (m_ref[...] + jnp.log2(jnp.maximum(l_all, 1e-37))).T
            rows = pl.ds(pl.multiple_of(c * CHUNK, CHUNK), CHUNK)
            lse = l_ref[rows, :]
            lse_ref[p, rows, :] = lse
            row_in[p, camp, rows, :] = lse

            @pl.when((p == 0) & (c == 0))
            def _():
                pl.semaphore_wait(barrier, (n_camp - 1) + (n_z - 1) + 1)

            for peer in camp_peers:
                row_copy(p, c, lse_ref, row_in, peer, camp).start()
            return 0

        lax.fori_loop(0, chunks, visit, 0, unroll=True)

        @pl.when(p == 0)
        def _():
            sel[...] = jnp.where(
                (lax.broadcasted_iota(jnp.int32, (col_blocks, wide), 0) == block_id)
                & (valid > 0),
                1.0,
                0.0,
            ).astype(BF16)

        def weigh(c, _):
            rows = pl.ds(pl.multiple_of(c * CHUNK, CHUNK), CHUNK)
            for peer in camp_peers[::-1]:
                row_copy(p, c, lse_ref, row_in, peer, peer).wait_recv()
            every = row_in[p, :, rows, :]
            top = jnp.maximum(jnp.max(every, axis=0), 0.0)
            total = jnp.exp2(-top) + jnp.sum(jnp.exp2(every - top[None]), axis=0)
            turn_ref[rows, :] = top + jnp.log2(total)
            weight = jnp.exp2(m_ref[...] - turn_ref[...].T)
            l_ref[...] = weight
            turned = pltpu.roll(weight, lax.rem(BLOCK - c * CHUNK, BLOCK), 1)
            first, second = [], []
            whi = turned.astype(BF16)
            wmid = (turned - whi.astype(F32)).astype(BF16)
            terms = jnp.concatenate([whi, wmid], axis=1)
            pair = lax.rem(lax.broadcasted_iota(jnp.int32, (BLOCK, 2 * BLOCK), 1), BLOCK) // 2
            ri = lax.broadcasted_iota(jnp.int32, (2 * BLOCK, 2 * BLOCK), 0)
            ci = lax.broadcasted_iota(jnp.int32, (2 * BLOCK, 2 * BLOCK), 1)
            spread = jnp.where(lax.rem(ri, 2) == ci // BLOCK, 1.0, 0.0).astype(BF16)
            for u in range(0, CHUNK, 2):
                w2 = mm(jnp.where(pair == u // 2, terms, jnp.zeros_like(terms)), spread)
                for v in range(2):
                    w = w2[:, v * BLOCK : (v + 1) * BLOCK]
                    e = e_ref[c * CHUNK + u + v]
                    first.append(jnp.sum(e[:, 0:BLOCK] * w, axis=0, keepdims=True))
                    second.append(jnp.sum(e[:, BLOCK:] * w, axis=0, keepdims=True))
            parts[rows, :] = jnp.concatenate(first, axis=0)
            parts[pl.ds(pl.multiple_of(row_blocks + c * CHUNK, CHUNK), CHUNK), :] = (
                jnp.concatenate(second, axis=0)
            )
            return 0

        lax.fori_loop(0, chunks, weigh, 0)

        def weigh_lead(k, _):
            place = place_of(k)
            w = jnp.sum(jnp.where(lane == place, l_ref[...], 0.0), axis=1, keepdims=True)
            part = jnp.sum(el_ref[k] * w, axis=0, keepdims=True)
            for s in range(LEAD_SLOTS):
                parts[pl.ds(2 * row_blocks + s * LEADS + k, 1), :] = part[
                    :, s * BLOCK : (s + 1) * BLOCK
                ]
            return 0

        lax.fori_loop(0, LEADS, weigh_lead, 0, unroll=4)

        cols[p] = exact_pick(sel[...], parts[...])
        for peer in z_peers:
            sib_copy(p, peer).start()
        sib_copy(p, z).start()
        for peer in z_peers:
            sib_copy(p, peer).wait_recv()
            z_out[p, peer] = cols[p, price_rows(core, peer), :] + sib_in[p, peer]
            z_copy(p, peer, z).start()
        sib_copy(p, z).wait_recv()
        here = price_rows(core, z)
        total = cols[p, here, :] + sib_in[p, z]
        for peer in z_peers[::-1]:
            z_copy(p, peer, peer).wait_recv()
            total = total + z_in[p, peer]
        prices[p + 1, here, :] = jnp.maximum(
            prices[p, here, :] + step_ref[p] * (total - spend_ref[here, :]), 0.0
        )
        for peer in z_peers:
            price_copy(p, peer, z).start()
        cross_copy(p, core, z).start()
        for peer in z_peers[::-1]:
            price_copy(p, peer, peer).wait_recv()
            cross_copy(p, core, peer).start()
        cross_copy(p, 1 - core, z).wait_recv()
        for peer in z_peers[::-1]:
            cross_copy(p, 1 - core, peer).wait_recv()
        return 0

    lax.fori_loop(0, PASSES, one_pass, 0)
    out_price[...] = prices[PASSES]
    out_norm[...] = turn_ref[0:row_blocks, :] * LN2

    def drain(p, _):
        def drain_rows(c, _):
            for peer in camp_peers:
                row_copy(p, c, lse_ref, row_in, peer, camp).wait_send()
            return 0

        lax.fori_loop(0, chunks, drain_rows, 0)
        for peer in z_peers:
            sib_copy(p, peer).wait_send()
            z_copy(p, peer, z).wait_send()
            price_copy(p, peer, z).wait_send()
            cross_copy(p, core, peer).wait_send()
        sib_copy(p, z).wait_send()
        cross_copy(p, core, z).wait_send()
        return 0

    lax.fori_loop(0, PASSES, drain, 0)


def local(
    n_dp, n_camp, row_factors, col_factors, prices, spend_target, step_sizes, eligible, counts
):
    row_blocks, slots = eligible.shape
    col_blocks = prices.shape[0] // BLOCK
    n_z = n_dp // 2
    side = math.isqrt(n_camp)
    chunk = col_blocks // 2 // n_z
    chunks = row_blocks // CHUNK
    wide = 256
    dma = pltpu.SemaphoreType.DMA
    vmem = pltpu.VMEM
    spec = pl.BlockSpec(memory_space=pltpu.VMEM)
    smem = pl.BlockSpec(memory_space=pltpu.SMEM)
    hbm = pl.BlockSpec(memory_space=pltpu.HBM)
    rows_t = row_factors.T
    index, tiles, lead_tiles, lead_rows = pl.pallas_call(
        functools.partial(gather_kernel, col_blocks),
        out_shape=(
            vmem((8, wide), jnp.int32),
            vmem((row_blocks, RANK, 2 * BLOCK), BF16),
            vmem((LEADS, RANK, LEAD_SLOTS * BLOCK), BF16),
            vmem((LEADS, RANK, BLOCK), BF16),
        ),
        in_specs=[hbm] * 4,
        out_specs=(spec,) * 4,
        scratch_shapes=[
            vmem((slots, row_blocks), jnp.int32),
            vmem((1, row_blocks), jnp.int32),
            vmem(rows_t.shape, BF16),
            vmem((RANK, col_blocks * BLOCK), BF16),
            pltpu.SMEM((8, wide), jnp.int32),
            dma((5,)),
        ],
        compiler_params=pltpu.CompilerParams(vmem_limit_bytes=60 * 1024 * 1024),
    )(eligible.T, counts.reshape(1, row_blocks), rows_t, col_factors.T)
    per_z = (PASSES, n_z, chunk, BLOCK)
    square = vmem((BLOCK, BLOCK), F32)
    new_prices, norms = pl.pallas_call(
        functools.partial(kernel, n_z, side),
        out_shape=(
            vmem((col_blocks, BLOCK), F32),
            vmem((row_blocks, BLOCK), F32),
        ),
        in_specs=[spec] * 6 + [smem, spec],
        out_specs=(spec, spec),
        scratch_shapes=[
            vmem((col_blocks, wide), BF16),
            vmem((wide, col_blocks), BF16),
            vmem((wide, BLOCK), F32),
            vmem((row_blocks, 2 * BLOCK), F32),
            vmem((LEADS, LEAD_SLOTS * BLOCK), F32),
            vmem((row_blocks, BLOCK, 2 * BLOCK), F32),
            vmem((LEADS, BLOCK, LEAD_SLOTS * BLOCK), F32),
            vmem((row_blocks, BLOCK, 2 * BLOCK), F32),
            vmem((LEADS, BLOCK, LEAD_SLOTS * BLOCK), F32),
            vmem((CHUNK, BLOCK, BLOCK), F32),
            vmem((LEADS, BLOCK, BLOCK), F32),
            square,
            square,
            square,
            square,
            square,
            vmem((PASSES, row_blocks, BLOCK), F32),
            vmem((PASSES, n_camp, row_blocks, BLOCK), F32),
            vmem((wide, BLOCK), F32),
            vmem((PASSES, col_blocks, BLOCK), F32),
            vmem(per_z, F32),
            vmem(per_z, F32),
            vmem(per_z, F32),
            vmem((PASSES + 1, col_blocks, BLOCK), F32),
            dma((PASSES, chunks, n_camp)),
            dma((PASSES, chunks, n_camp)),
        ]
        + [dma((PASSES, n_z))] * 8,
        compiler_params=pltpu.CompilerParams(
            collective_id=0, has_side_effects=True, vmem_limit_bytes=48 * 1024 * 1024
        ),
    )(
        rows_t,
        tiles,
        lead_tiles,
        lead_rows,
        prices.reshape(col_blocks, BLOCK),
        spend_target.reshape(col_blocks, BLOCK),
        step_sizes,
        index,
    )
    return new_prices.reshape(-1), norms.reshape(-1)


def solution(mesh):
    placed = (P("dp", None), P("camp", None), P("camp"), P("camp"), P(), P("dp", None), P("dp"))
    return jax.shard_map(
        functools.partial(local, mesh.shape["dp"], mesh.shape["camp"]),
        mesh=mesh,
        in_specs=placed,
        out_specs=(P("camp"), P("dp")),
        check_vma=False,
    )
```

```python
import functools
import math

import jax
import jax.numpy as jnp
from jax import lax
from jax.experimental import pallas as pl
from jax.experimental.pallas import tpu as pltpu
from jax.sharding import PartitionSpec as P

MESH = pl.DeviceIdType.MESH
F32 = jnp.float32
BF16 = jnp.bfloat16
BLOCK = 128
RANK = 32
PASSES = 3
LEADS = 8
LEAD_SLOTS = 8
SCALE = math.log2(math.e) / 0.3
LN2 = math.log(2.0)
DEAD = 1e30
CHUNK = 32


def pieces(x):
    hi = x.astype(BF16)
    rest = x - hi.astype(F32)
    mid = rest.astype(BF16)
    low = (rest - mid.astype(F32)).astype(BF16)
    return hi, mid, low


def mm(a, b):
    return lax.dot_general(a, b, (((1,), (0,)), ((), ())), preferred_element_type=F32)


def mm_tn(a, b):
    return lax.dot_general(a, b, (((0,), (0,)), ((), ())), preferred_element_type=F32)


def mm_nt(a, b):
    return lax.dot_general(a, b, (((1,), (1,)), ((), ())), preferred_element_type=F32)


def exact_pick(select, x):
    return pick_terms(select, jnp.concatenate(pieces(x), axis=1))


def pick_terms(select, terms):
    out = mm(select, terms)
    return out[:, :BLOCK] + out[:, BLOCK : 2 * BLOCK] + out[:, 2 * BLOCK :]


def slot_index(elig, cnt, own, col_blocks):
    slots, rows = elig.shape
    pos = lax.broadcasted_iota(jnp.int32, elig.shape, 0)
    owned = lax.div(elig, col_blocks) == own
    led = owned[0:1, :]
    first = jnp.min(jnp.where(owned, pos, slots), axis=0, keepdims=True)
    blocks, valids = [], []
    for k in range(2):
        picked = first + k
        chosen = jnp.sum(jnp.where(pos == picked, elig, 0), axis=0, keepdims=True)
        ok = (
            (picked < slots)
            & (lax.div(chosen, col_blocks) == own)
            & (picked < cnt)
            & jnp.logical_not(led)
        )
        blocks.append(jnp.where(ok, chosen - own * col_blocks, 0))
        valids.append(ok.astype(jnp.int32))
    led_f = jnp.broadcast_to(led.astype(F32), (8, rows))
    before = (
        lax.broadcasted_iota(jnp.int32, (rows, rows), 0)
        < lax.broadcasted_iota(jnp.int32, (rows, rows), 1)
    ).astype(F32)
    rank = mm(led_f.astype(BF16), before.astype(BF16))[0:1, :]
    lane = lax.broadcasted_iota(jnp.int32, (LEADS * LEAD_SLOTS, rows), 0)
    hot = jnp.where((rank == lax.rem(lane, LEADS).astype(F32)) & led, 1.0, 0.0)
    row_id = lax.broadcasted_iota(jnp.int32, (8, rows), 1).astype(F32)
    high = lax.div(elig, 128)
    picked = mm_nt(
        jnp.concatenate(
            [
                high.astype(F32),
                (elig - high * 128).astype(F32),
                jnp.broadcast_to(cnt, (8, rows)).astype(F32),
                jnp.ones((8, rows), F32),
                row_id,
            ],
            axis=0,
        ).astype(BF16),
        hot.astype(BF16),
    )
    wide = LEADS * LEAD_SLOTS
    every = picked[0:slots] * 128.0 + picked[slots : 2 * slots]
    slot_of = lax.div(lax.broadcasted_iota(jnp.int32, (slots, wide), 1), LEADS)
    chosen = jnp.sum(
        jnp.where(lax.broadcasted_iota(jnp.int32, (slots, wide), 0) == slot_of, every, 0.0),
        axis=0,
        keepdims=True,
    ).astype(jnp.int32)
    lead_cnt = picked[2 * slots : 2 * slots + 1]
    exists = picked[2 * slots + 8 : 2 * slots + 9] > 0.5
    lead_row = picked[2 * slots + 16 : 2 * slots + 17].astype(jnp.int32)
    ok = exists & (slot_of[0:1].astype(F32) < lead_cnt)
    blocks.append(jnp.where(ok, chosen - own * col_blocks, 0))
    valids.append(ok.astype(jnp.int32))
    blocks.append(jnp.zeros_like(lead_row))
    valids.append(jnp.zeros_like(lead_row))
    place = jnp.where(exists, lead_row, -1)
    return (
        jnp.concatenate(blocks, axis=1),
        jnp.concatenate(valids, axis=1),
        jnp.concatenate([lead_row, place, lead_row, place], axis=1),
    )


def gather_kernel(
    col_blocks,
    elig_hbm,
    cnt_hbm,
    row_hbm,
    col_hbm,
    index_out,
    tiles_out,
    lead_tiles_out,
    lead_rows_out,
    elig_ref,
    cnt_ref,
    row_ref,
    col_ref,
    index_s,
    sem,
):
    loads = [
        pltpu.make_async_copy(src, dst, sem.at[i])
        for i, (src, dst) in enumerate(
            ((elig_hbm, elig_ref), (cnt_hbm, cnt_ref), (col_hbm, col_ref), (row_hbm, row_ref))
        )
    ]
    for load in loads:
        load.start()
    own = lax.axis_index("camp")
    loads[0].wait()
    loads[1].wait()
    block_id, valid, lead_info = slot_index(elig_ref[...], cnt_ref[...], own, col_blocks)
    rest = jnp.zeros((5, block_id.shape[1]), jnp.int32)
    index_out[...] = jnp.concatenate([block_id, valid, lead_info, rest], axis=0)
    to_smem = pltpu.make_async_copy(index_out, index_s, sem.at[4])
    to_smem.start()
    to_smem.wait()
    loads[2].wait()
    row_blocks = tiles_out.shape[0]

    def pick(t):
        return col_ref[:, pl.ds(pl.multiple_of(index_s[0, t] * BLOCK, BLOCK), BLOCK)]

    def regular(b, _):
        tiles_out[b, :, 0:BLOCK] = pick(b)
        tiles_out[b, :, BLOCK : 2 * BLOCK] = pick(row_blocks + b)
        return 0

    lax.fori_loop(0, row_blocks, regular, 0, unroll=8)
    loads[3].wait()

    def lead(k, _):
        for s in range(LEAD_SLOTS):
            lead_tiles_out[k, :, s * BLOCK : (s + 1) * BLOCK] = pick(
                2 * row_blocks + s * LEADS + k
            )
        at = pl.multiple_of(index_s[2, k] * BLOCK, BLOCK)
        lead_rows_out[k] = row_ref[:, pl.ds(at, BLOCK)]
        return 0

    lax.fori_loop(0, LEADS, lead, 0, unroll=2)


def far_first(side):
    return sorted(range(1, side), key=lambda k: -min(k, side - k))


def kernel(
    n_z,
    side,
    row_ref,
    tile_ref,
    lead_tile_ref,
    lead_row_ref,
    price_ref,
    spend_ref,
    step_ref,
    idx_ref,
    out_price,
    out_norm,
    sel,
    selt,
    bias,
    pg,
    pgl,
    s_ref,
    sl_ref,
    e_ref,
    el_ref,
    sum_ref,
    lead_sum_ref,
    m_ref,
    l_ref,
    ml_ref,
    ll_ref,
    turn_ref,
    lse_ref,
    row_in,
    parts,
    cols,
    sib_in,
    z_out,
    z_in,
    prices,
    row_send,
    row_recv,
    sib_send,
    sib_recv,
    z_send,
    z_recv,
    pz_send,
    pz_recv,
    pc_send,
    pc_recv,
):
    dp = lax.axis_index("dp")
    camp = lax.axis_index("camp")
    z = lax.div(dp, 2)
    core = lax.rem(dp, 2)
    x = lax.div(camp, side)
    y = lax.rem(camp, side)
    sibling = 2 * z + 1 - core
    row_blocks = s_ref.shape[0]
    chunks = row_blocks // CHUNK
    col_blocks = spend_ref.shape[0]
    half = col_blocks // 2
    chunk = half // n_z
    n_camp = side * side

    hops = [min(k, side - k) for k in range(side)]
    camp_peers = [
        lax.rem(x + dx, side) * side + lax.rem(y + dy, side)
        for dx, dy in sorted(
            ((a, b) for a in range(side) for b in range(side) if a or b),
            key=lambda ab: -hops[ab[0]] - hops[ab[1]],
        )
    ]
    z_peers = [lax.rem(z + k, n_z) for k in far_first(n_z)]

    barrier = pltpu.get_barrier_semaphore()
    for peer in camp_peers:
        pl.semaphore_signal(barrier, inc=1, device_id=(dp, peer), device_id_type=MESH)
    for peer in z_peers:
        pl.semaphore_signal(
            barrier, inc=1, device_id=(2 * peer + core, camp), device_id_type=MESH
        )
    pl.semaphore_signal(barrier, inc=1, device_id=(sibling, camp), device_id_type=MESH)

    block_id = idx_ref[0:1, :]
    valid = idx_ref[1:2, :]
    wide = block_id.shape[1]
    both = jnp.concatenate(
        [block_id.astype(F32), valid.astype(F32), jnp.zeros((6, wide), F32)], axis=0
    )
    for half_t in range(2):
        part = both[:, half_t * BLOCK : (half_t + 1) * BLOCK]
        turned = jnp.concatenate([part, jnp.zeros((BLOCK - 8, BLOCK), F32)], axis=0).T
        at = turned[:, 0:1]
        ok = turned[:, 1:2]
        lanes = lax.broadcasted_iota(jnp.int32, (BLOCK, col_blocks), 1).astype(F32)
        selt[half_t * BLOCK : (half_t + 1) * BLOCK, :] = jnp.where(
            (lanes == at) & (ok > 0.5), 1.0, 0.0
        ).astype(BF16)
        bias[half_t * BLOCK : (half_t + 1) * BLOCK, :] = jnp.broadcast_to(
            jnp.where(ok > 0.5, 0.0, DEAD), (BLOCK, BLOCK)
        )

    def score(b, _):
        at = pl.multiple_of(b * BLOCK, BLOCK)
        s_ref[b] = mm_tn(row_ref[:, pl.ds(at, BLOCK)], tile_ref[b]) * SCALE
        return 0

    lax.fori_loop(0, row_blocks, score, 0, unroll=32)

    def score_lead(k, _):
        sl_ref[k] = mm_tn(lead_row_ref[k], lead_tile_ref[k]) * SCALE
        return 0

    lax.fori_loop(0, LEADS, score_lead, 0, unroll=8)

    parts[...] = jnp.zeros_like(parts)
    turn_ref[...] = jnp.zeros_like(turn_ref)
    prices[0] = price_ref[...]

    lane = lax.broadcasted_iota(jnp.int32, (BLOCK, BLOCK), 1)

    def place_of(k):
        places = idx_ref[2:3, 0:BLOCK]
        at = lax.broadcasted_iota(jnp.int32, (1, BLOCK), 1) == LEADS * LEAD_SLOTS + k
        return jnp.sum(jnp.where(at, places, 0), axis=1, keepdims=True)

    def price_rows(of_core, peer):
        return pl.ds(pl.multiple_of(of_core * half + peer * chunk, chunk), chunk)

    def row_copy(p, c, src, dst, peer, slot):
        rows = pl.ds(pl.multiple_of(c * CHUNK, CHUNK), CHUNK)
        return pltpu.make_async_remote_copy(
            src_ref=src.at[p, rows],
            dst_ref=dst.at[p, slot, rows],
            send_sem=row_send.at[p, c, peer],
            recv_sem=row_recv.at[p, c, slot],
            device_id=(dp, peer),
            device_id_type=MESH,
        )

    def sib_copy(p, peer):
        return pltpu.make_async_remote_copy(
            src_ref=cols.at[p, price_rows(1 - core, peer)],
            dst_ref=sib_in.at[p, peer],
            send_sem=sib_send.at[p, peer],
            recv_sem=sib_recv.at[p, peer],
            device_id=(sibling, camp),
            device_id_type=MESH,
        )

    def z_copy(p, peer, slot):
        return pltpu.make_async_remote_copy(
            src_ref=z_out.at[p, peer],
            dst_ref=z_in.at[p, slot],
            send_sem=z_send.at[p, peer],
            recv_sem=z_recv.at[p, slot],
            device_id=(2 * peer + core, camp),
            device_id_type=MESH,
        )

    def price_copy(p, peer, owner):
        rows = price_rows(core, owner)
        return pltpu.make_async_remote_copy(
            src_ref=prices.at[p + 1, rows],
            dst_ref=prices.at[p + 1, rows],
            send_sem=pz_send.at[p, peer],
            recv_sem=pz_recv.at[p, owner],
            device_id=(2 * peer + core, camp),
            device_id_type=MESH,
        )

    def cross_copy(p, of_core, owner):
        rows = price_rows(of_core, owner)
        return pltpu.make_async_remote_copy(
            src_ref=prices.at[p + 1, rows],
            dst_ref=prices.at[p + 1, rows],
            send_sem=pc_send.at[p, owner],
            recv_sem=pc_recv.at[p, owner],
            device_id=(sibling, camp),
            device_id_type=MESH,
        )

    def drain(p):
        for c in range(chunks):
            for peer in camp_peers:
                row_copy(p, c, lse_ref, row_in, peer, camp).wait_send()
        for peer in z_peers:
            sib_copy(p, peer).wait_send()
            z_copy(p, peer, z).wait_send()
        sib_copy(p, z).wait_send()

    def drain_prices(p):
        for peer in z_peers:
            price_copy(p, peer, z).wait_send()
            cross_copy(p, core, peer).wait_send()
        cross_copy(p, core, z).wait_send()

    def one_pass(p, _):
        picked = exact_pick(selt[...], prices[p] * SCALE) + bias[...]
        pg[:, 0:BLOCK] = picked[0:row_blocks]
        pg[:, BLOCK : 2 * BLOCK] = picked[row_blocks : 2 * row_blocks]
        for s in range(LEAD_SLOTS):
            base = 2 * row_blocks + s * LEADS
            pgl[:, s * BLOCK : (s + 1) * BLOCK] = picked[base : base + LEADS]
        ml_ref[...] = jnp.zeros_like(ml_ref)
        ll_ref[...] = jnp.zeros_like(ll_ref)

        def visit_lead(k, _):
            place = place_of(k)
            price = pgl[pl.ds(k, 1), :]
            for r in range(0, BLOCK, 32):
                logit = sl_ref[k, r : r + 32, :] - price
                top = logit[:, 0:BLOCK]
                for s in range(1, LEAD_SLOTS):
                    top = jnp.maximum(top, logit[:, s * BLOCK : (s + 1) * BLOCK])
                m = jnp.maximum(jnp.max(top, axis=1, keepdims=True), 0.0)
                e = jnp.exp2(logit - m)
                el_ref[k, r : r + 32, :] = e
                total = e[:, 0:BLOCK]
                for s in range(1, LEAD_SLOTS):
                    total = total + e[:, s * BLOCK : (s + 1) * BLOCK]
                lead_sum_ref[k, r : r + 32, :] = total
                ml_ref[r : r + 32, :] = jnp.where(
                    lane[r : r + 32] == place, m, ml_ref[r : r + 32, :]
                )
            return 0

        lax.fori_loop(0, LEADS, visit_lead, 0, unroll=8)

        def add_lead(k, _):
            place = place_of(k)
            l = jnp.sum(lead_sum_ref[k], axis=1, keepdims=True)
            ll_ref[...] = jnp.where(lane == place, l, ll_ref[...])
            return 0

        lax.fori_loop(0, LEADS, add_lead, 0, unroll=8)
        m_ref[...] = ml_ref[...]

        def visit(c, _):
            m_all = jnp.zeros((BLOCK, BLOCK), F32)
            l_all = jnp.zeros((BLOCK, BLOCK), F32)
            for u in range(CHUNK):
                b = c * CHUNK + u
                logit = s_ref[b] - pg[pl.ds(b, 1), :]
                top = jnp.maximum(logit[:, 0:BLOCK], logit[:, BLOCK:])
                m = jnp.maximum(jnp.max(top, axis=1, keepdims=True), 0.0)
                e = jnp.exp2(logit - m)
                e_ref[b] = e
                sum_ref[u] = e[:, 0:BLOCK] + e[:, BLOCK:]
                m_all = jnp.where(lane == b, m, m_all)
                if u >= 2:
                    l = jnp.sum(sum_ref[u - 2], axis=1, keepdims=True)
                    l_all = jnp.where(lane == b - 2, l, l_all)
            for u in range(CHUNK - 2, CHUNK):
                l = jnp.sum(sum_ref[u], axis=1, keepdims=True)
                l_all = jnp.where(lane == c * CHUNK + u, l, l_all)
            m_ref[...] = m_ref[...] + m_all
            l_all = l_all + ll_ref[...]
            l_ref[...] = (m_ref[...] + jnp.log2(jnp.maximum(l_all, 1e-37))).T
            rows = pl.ds(pl.multiple_of(c * CHUNK, CHUNK), CHUNK)
            lse = l_ref[rows, :]
            lse_ref[p, rows, :] = lse
            row_in[p, camp, rows, :] = lse

            @pl.when((p == 0) & (c == 0))
            def _():
                pl.semaphore_wait(barrier, (n_camp - 1) + (n_z - 1) + 1)

            for peer in camp_peers:
                row_copy(p, c, lse_ref, row_in, peer, camp).start()
            return 0

        lax.fori_loop(0, chunks, visit, 0, unroll=True)

        @pl.when(p > 0)
        def _():
            drain_prices(p - 1)

        @pl.when(p == 0)
        def _():
            sel[...] = jnp.where(
                (lax.broadcasted_iota(jnp.int32, (col_blocks, wide), 0) == block_id)
                & (valid > 0),
                1.0,
                0.0,
            ).astype(BF16)

        def weigh(c, _):
            rows = pl.ds(pl.multiple_of(c * CHUNK, CHUNK), CHUNK)
            for peer in camp_peers[::-1]:
                row_copy(p, c, lse_ref, row_in, peer, peer).wait_recv()
            every = row_in[p, :, rows, :]
            top = jnp.maximum(jnp.max(every, axis=0), 0.0)
            total = jnp.exp2(-top) + jnp.sum(jnp.exp2(every - top[None]), axis=0)
            turn_ref[rows, :] = top + jnp.log2(total)
            weight = jnp.exp2(m_ref[...] - turn_ref[...].T)
            l_ref[...] = weight
            turned = pltpu.roll(weight, lax.rem(BLOCK - c * CHUNK, BLOCK), 1)
            first, second = [], []
            whi = turned.astype(BF16)
            wmid = (turned - whi.astype(F32)).astype(BF16)
            terms = jnp.concatenate([whi, wmid], axis=1)
            pair = lax.rem(lax.broadcasted_iota(jnp.int32, (BLOCK, 2 * BLOCK), 1), BLOCK) // 2
            ri = lax.broadcasted_iota(jnp.int32, (2 * BLOCK, 2 * BLOCK), 0)
            ci = lax.broadcasted_iota(jnp.int32, (2 * BLOCK, 2 * BLOCK), 1)
            spread = jnp.where(lax.rem(ri, 2) == ci // BLOCK, 1.0, 0.0).astype(BF16)
            for u in range(0, CHUNK, 2):
                w2 = mm(jnp.where(pair == u // 2, terms, jnp.zeros_like(terms)), spread)
                for v in range(2):
                    w = w2[:, v * BLOCK : (v + 1) * BLOCK]
                    e = e_ref[c * CHUNK + u + v]
                    first.append(jnp.sum(e[:, 0:BLOCK] * w, axis=0, keepdims=True))
                    second.append(jnp.sum(e[:, BLOCK:] * w, axis=0, keepdims=True))
            parts[rows, :] = jnp.concatenate(first, axis=0)
            parts[pl.ds(pl.multiple_of(row_blocks + c * CHUNK, CHUNK), CHUNK), :] = (
                jnp.concatenate(second, axis=0)
            )
            return 0

        for c in range(chunks):
            weigh(c, 0)

        def weigh_lead(k, _):
            place = place_of(k)
            w = jnp.sum(jnp.where(lane == place, l_ref[...], 0.0), axis=1, keepdims=True)
            part = jnp.sum(el_ref[k] * w, axis=0, keepdims=True)
            for s in range(LEAD_SLOTS):
                parts[pl.ds(2 * row_blocks + s * LEADS + k, 1), :] = part[
                    :, s * BLOCK : (s + 1) * BLOCK
                ]
            return 0

        for k in range(LEADS):
            weigh_lead(k, 0)

        terms = jnp.concatenate(pieces(parts[...]), axis=1)
        away = pl.ds(pl.multiple_of((1 - core) * half, half), half)
        home = pl.ds(pl.multiple_of(core * half, half), half)
        cols[p, away, :] = pick_terms(sel[away, :], terms)
        for peer in z_peers:
            sib_copy(p, peer).start()
        sib_copy(p, z).start()
        cols[p, home, :] = pick_terms(sel[home, :], terms)
        for peer in z_peers:
            sib_copy(p, peer).wait_recv()
            z_out[p, peer] = cols[p, price_rows(core, peer), :] + sib_in[p, peer]
            z_copy(p, peer, z).start()
        sib_copy(p, z).wait_recv()
        here = price_rows(core, z)
        total = cols[p, here, :] + sib_in[p, z]
        for peer in z_peers[::-1]:
            z_copy(p, peer, peer).wait_recv()
            total = total + z_in[p, peer]
        prices[p + 1, here, :] = jnp.maximum(
            prices[p, here, :] + step_ref[p] * (total - spend_ref[here, :]), 0.0
        )
        for peer in z_peers:
            price_copy(p, peer, z).start()
        cross_copy(p, core, z).start()
        drain(p)
        for peer in z_peers[::-1]:
            price_copy(p, peer, peer).wait_recv()
            cross_copy(p, core, peer).start()
        cross_copy(p, 1 - core, z).wait_recv()
        for peer in z_peers[::-1]:
            cross_copy(p, 1 - core, peer).wait_recv()
        return 0

    lax.fori_loop(0, PASSES, one_pass, 0)
    out_price[...] = prices[PASSES]
    out_norm[...] = turn_ref[0:row_blocks, :] * LN2

    drain_prices(PASSES - 1)


def local(
    n_dp, n_camp, row_factors, col_factors, prices, spend_target, step_sizes, eligible, counts
):
    row_blocks, slots = eligible.shape
    col_blocks = prices.shape[0] // BLOCK
    n_z = n_dp // 2
    side = math.isqrt(n_camp)
    chunk = col_blocks // 2 // n_z
    chunks = row_blocks // CHUNK
    wide = 256
    dma = pltpu.SemaphoreType.DMA
    vmem = pltpu.VMEM
    spec = pl.BlockSpec(memory_space=pltpu.VMEM)
    smem = pl.BlockSpec(memory_space=pltpu.SMEM)
    hbm = pl.BlockSpec(memory_space=pltpu.HBM)
    rows_t = row_factors.T
    index, tiles, lead_tiles, lead_rows = pl.pallas_call(
        functools.partial(gather_kernel, col_blocks),
        out_shape=(
            vmem((8, wide), jnp.int32),
            vmem((row_blocks, RANK, 2 * BLOCK), BF16),
            vmem((LEADS, RANK, LEAD_SLOTS * BLOCK), BF16),
            vmem((LEADS, RANK, BLOCK), BF16),
        ),
        in_specs=[hbm] * 4,
        out_specs=(spec,) * 4,
        scratch_shapes=[
            vmem((slots, row_blocks), jnp.int32),
            vmem((1, row_blocks), jnp.int32),
            vmem(rows_t.shape, BF16),
            vmem((RANK, col_blocks * BLOCK), BF16),
            pltpu.SMEM((8, wide), jnp.int32),
            dma((5,)),
        ],
        compiler_params=pltpu.CompilerParams(vmem_limit_bytes=60 * 1024 * 1024),
    )(eligible.T, counts.reshape(1, row_blocks), rows_t, col_factors.T)
    per_z = (PASSES, n_z, chunk, BLOCK)
    square = vmem((BLOCK, BLOCK), F32)
    new_prices, norms = pl.pallas_call(
        functools.partial(kernel, n_z, side),
        out_shape=(
            vmem((col_blocks, BLOCK), F32),
            vmem((row_blocks, BLOCK), F32),
        ),
        in_specs=[spec] * 6 + [smem, spec],
        out_specs=(spec, spec),
        scratch_shapes=[
            vmem((col_blocks, wide), BF16),
            vmem((wide, col_blocks), BF16),
            vmem((wide, BLOCK), F32),
            vmem((row_blocks, 2 * BLOCK), F32),
            vmem((LEADS, LEAD_SLOTS * BLOCK), F32),
            vmem((row_blocks, BLOCK, 2 * BLOCK), F32),
            vmem((LEADS, BLOCK, LEAD_SLOTS * BLOCK), F32),
            vmem((row_blocks, BLOCK, 2 * BLOCK), F32),
            vmem((LEADS, BLOCK, LEAD_SLOTS * BLOCK), F32),
            vmem((CHUNK, BLOCK, BLOCK), F32),
            vmem((LEADS, BLOCK, BLOCK), F32),
            square,
            square,
            square,
            square,
            square,
            vmem((PASSES, row_blocks, BLOCK), F32),
            vmem((PASSES, n_camp, row_blocks, BLOCK), F32),
            vmem((wide, BLOCK), F32),
            vmem((PASSES, col_blocks, BLOCK), F32),
            vmem(per_z, F32),
            vmem(per_z, F32),
            vmem(per_z, F32),
            vmem((PASSES + 1, col_blocks, BLOCK), F32),
            dma((PASSES, chunks, n_camp)),
            dma((PASSES, chunks, n_camp)),
        ]
        + [dma((PASSES, n_z))] * 8,
        compiler_params=pltpu.CompilerParams(
            collective_id=0, has_side_effects=True, vmem_limit_bytes=48 * 1024 * 1024
        ),
    )(
        rows_t,
        tiles,
        lead_tiles,
        lead_rows,
        prices.reshape(col_blocks, BLOCK),
        spend_target.reshape(col_blocks, BLOCK),
        step_sizes,
        index,
    )
    return new_prices.reshape(-1), norms.reshape(-1)


def solution(mesh):
    placed = (P("dp", None), P("camp", None), P("camp"), P("camp"), P(), P("dp", None), P("dp"))
    return jax.shard_map(
        functools.partial(local, mesh.shape["dp"], mesh.shape["camp"]),
        mesh=mesh,
        in_specs=placed,
        out_specs=(P("camp"), P("dp")),
        check_vma=False,
    )
```

```python
import functools
import math

import jax
import jax.numpy as jnp
from jax import lax
from jax.experimental import pallas as pl
from jax.experimental.pallas import tpu as pltpu
from jax.sharding import PartitionSpec as P

MESH = pl.DeviceIdType.MESH
F32 = jnp.float32
BF16 = jnp.bfloat16
BLOCK = 128
RANK = 32
PASSES = 3
LEADS = 8
LEAD_SLOTS = 8
SCALE = math.log2(math.e) / 0.3
LN2 = math.log(2.0)
DEAD = 1e30
CHUNKS = ((0, 24), (24, 40))


def pieces(x):
    hi = x.astype(BF16)
    rest = x - hi.astype(F32)
    mid = rest.astype(BF16)
    low = (rest - mid.astype(F32)).astype(BF16)
    return hi, mid, low


def mm(a, b):
    return lax.dot_general(a, b, (((1,), (0,)), ((), ())), preferred_element_type=F32)


def mm_tn(a, b):
    return lax.dot_general(a, b, (((0,), (0,)), ((), ())), preferred_element_type=F32)


def mm_nt(a, b):
    return lax.dot_general(a, b, (((1,), (1,)), ((), ())), preferred_element_type=F32)


def exact_pick(select, x):
    return pick_terms(select, jnp.concatenate(pieces(x), axis=1))


def pick_terms(select, terms):
    out = mm(select, terms)
    return out[:, :BLOCK] + out[:, BLOCK : 2 * BLOCK] + out[:, 2 * BLOCK :]


def slot_index(elig, cnt, own, col_blocks):
    slots, rows = elig.shape
    pos = lax.broadcasted_iota(jnp.int32, elig.shape, 0)
    owned = lax.div(elig, col_blocks) == own
    led = owned[0:1, :]
    first = jnp.min(jnp.where(owned, pos, slots), axis=0, keepdims=True)
    blocks, valids = [], []
    for k in range(2):
        picked = first + k
        chosen = jnp.sum(jnp.where(pos == picked, elig, 0), axis=0, keepdims=True)
        ok = (
            (picked < slots)
            & (lax.div(chosen, col_blocks) == own)
            & (picked < cnt)
            & jnp.logical_not(led)
        )
        blocks.append(jnp.where(ok, chosen - own * col_blocks, 0))
        valids.append(ok.astype(jnp.int32))
    led_f = jnp.broadcast_to(led.astype(F32), (8, rows))
    before = (
        lax.broadcasted_iota(jnp.int32, (rows, rows), 0)
        < lax.broadcasted_iota(jnp.int32, (rows, rows), 1)
    ).astype(F32)
    rank = mm(led_f.astype(BF16), before.astype(BF16))[0:1, :]
    lane = lax.broadcasted_iota(jnp.int32, (LEADS * LEAD_SLOTS, rows), 0)
    hot = jnp.where((rank == lax.rem(lane, LEADS).astype(F32)) & led, 1.0, 0.0)
    row_id = lax.broadcasted_iota(jnp.int32, (8, rows), 1).astype(F32)
    high = lax.div(elig, 128)
    picked = mm_nt(
        jnp.concatenate(
            [
                high.astype(F32),
                (elig - high * 128).astype(F32),
                jnp.broadcast_to(cnt, (8, rows)).astype(F32),
                jnp.ones((8, rows), F32),
                row_id,
            ],
            axis=0,
        ).astype(BF16),
        hot.astype(BF16),
    )
    wide = LEADS * LEAD_SLOTS
    every = picked[0:slots] * 128.0 + picked[slots : 2 * slots]
    slot_of = lax.div(lax.broadcasted_iota(jnp.int32, (slots, wide), 1), LEADS)
    chosen = jnp.sum(
        jnp.where(lax.broadcasted_iota(jnp.int32, (slots, wide), 0) == slot_of, every, 0.0),
        axis=0,
        keepdims=True,
    ).astype(jnp.int32)
    lead_cnt = picked[2 * slots : 2 * slots + 1]
    exists = picked[2 * slots + 8 : 2 * slots + 9] > 0.5
    lead_row = picked[2 * slots + 16 : 2 * slots + 17].astype(jnp.int32)
    ok = exists & (slot_of[0:1].astype(F32) < lead_cnt)
    blocks.append(jnp.where(ok, chosen - own * col_blocks, 0))
    valids.append(ok.astype(jnp.int32))
    blocks.append(jnp.zeros_like(lead_row))
    valids.append(jnp.zeros_like(lead_row))
    place = jnp.where(exists, lead_row, -1)
    return (
        jnp.concatenate(blocks, axis=1),
        jnp.concatenate(valids, axis=1),
        jnp.concatenate([lead_row, place, lead_row, place], axis=1),
    )


def gather_kernel(
    col_blocks,
    elig_hbm,
    cnt_hbm,
    row_hbm,
    col_hbm,
    index_out,
    tiles_out,
    lead_tiles_out,
    lead_rows_out,
    elig_ref,
    cnt_ref,
    row_ref,
    col_ref,
    index_s,
    sem,
):
    loads = [
        pltpu.make_async_copy(src, dst, sem.at[i])
        for i, (src, dst) in enumerate(
            ((elig_hbm, elig_ref), (cnt_hbm, cnt_ref), (col_hbm, col_ref), (row_hbm, row_ref))
        )
    ]
    for load in loads:
        load.start()
    own = lax.axis_index("camp")
    loads[0].wait()
    loads[1].wait()
    block_id, valid, lead_info = slot_index(elig_ref[...], cnt_ref[...], own, col_blocks)
    rest = jnp.zeros((5, block_id.shape[1]), jnp.int32)
    index_out[...] = jnp.concatenate([block_id, valid, lead_info, rest], axis=0)
    to_smem = pltpu.make_async_copy(index_out, index_s, sem.at[4])
    to_smem.start()
    to_smem.wait()
    loads[2].wait()
    row_blocks = tiles_out.shape[0]

    def pick(t):
        return col_ref[:, pl.ds(pl.multiple_of(index_s[0, t] * BLOCK, BLOCK), BLOCK)]

    def regular(b, _):
        tiles_out[b, :, 0:BLOCK] = pick(b)
        tiles_out[b, :, BLOCK : 2 * BLOCK] = pick(row_blocks + b)
        return 0

    lax.fori_loop(0, row_blocks, regular, 0, unroll=8)
    loads[3].wait()

    def lead(k, _):
        for s in range(LEAD_SLOTS):
            lead_tiles_out[k, :, s * BLOCK : (s + 1) * BLOCK] = pick(
                2 * row_blocks + s * LEADS + k
            )
        at = pl.multiple_of(index_s[2, k] * BLOCK, BLOCK)
        lead_rows_out[k] = row_ref[:, pl.ds(at, BLOCK)]
        return 0

    lax.fori_loop(0, LEADS, lead, 0, unroll=2)


def far_first(side):
    return sorted(range(1, side), key=lambda k: -min(k, side - k))


def kernel(
    n_z,
    side,
    row_ref,
    tile_ref,
    lead_tile_ref,
    lead_row_ref,
    price_ref,
    spend_ref,
    step_ref,
    idx_ref,
    out_price,
    out_norm,
    sel,
    selt,
    bias,
    pg,
    pgl,
    s_ref,
    sl_ref,
    e_ref,
    el_ref,
    sum_ref,
    lead_sum_ref,
    m_ref,
    l_ref,
    ml_ref,
    ll_ref,
    turn_ref,
    lse_ref,
    row_in,
    parts,
    cols,
    sib_in,
    z_out,
    z_in,
    prices,
    row_send,
    row_recv,
    sib_send,
    sib_recv,
    z_send,
    z_recv,
    pz_send,
    pz_recv,
    pc_send,
    pc_recv,
):
    dp = lax.axis_index("dp")
    camp = lax.axis_index("camp")
    z = lax.div(dp, 2)
    core = lax.rem(dp, 2)
    x = lax.div(camp, side)
    y = lax.rem(camp, side)
    sibling = 2 * z + 1 - core
    row_blocks = s_ref.shape[0]
    chunks = len(CHUNKS)
    col_blocks = spend_ref.shape[0]
    half = col_blocks // 2
    chunk = half // n_z
    n_camp = side * side

    hops = [min(k, side - k) for k in range(side)]
    camp_peers = [
        lax.rem(x + dx, side) * side + lax.rem(y + dy, side)
        for dx, dy in sorted(
            ((a, b) for a in range(side) for b in range(side) if a or b),
            key=lambda ab: -hops[ab[0]] - hops[ab[1]],
        )
    ]
    z_peers = [lax.rem(z + k, n_z) for k in far_first(n_z)]

    barrier = pltpu.get_barrier_semaphore()
    for peer in z_peers[0:1]:
        pl.semaphore_signal(
            barrier, inc=1, device_id=(2 * peer + core, camp), device_id_type=MESH
        )
    for peer in camp_peers:
        pl.semaphore_signal(barrier, inc=1, device_id=(dp, peer), device_id_type=MESH)
    for peer in z_peers[1:]:
        pl.semaphore_signal(
            barrier, inc=1, device_id=(2 * peer + core, camp), device_id_type=MESH
        )
    pl.semaphore_signal(barrier, inc=1, device_id=(sibling, camp), device_id_type=MESH)

    block_id = idx_ref[0:1, :]
    valid = idx_ref[1:2, :]
    wide = block_id.shape[1]
    both = jnp.concatenate(
        [block_id.astype(F32), valid.astype(F32), jnp.zeros((6, wide), F32)], axis=0
    )
    for half_t in range(2):
        part = both[:, half_t * BLOCK : (half_t + 1) * BLOCK]
        turned = jnp.concatenate([part, jnp.zeros((BLOCK - 8, BLOCK), F32)], axis=0).T
        at = turned[:, 0:1]
        ok = turned[:, 1:2]
        lanes = lax.broadcasted_iota(jnp.int32, (BLOCK, col_blocks), 1).astype(F32)
        selt[half_t * BLOCK : (half_t + 1) * BLOCK, :] = jnp.where(
            (lanes == at) & (ok > 0.5), 1.0, 0.0
        ).astype(BF16)
        bias[half_t * BLOCK : (half_t + 1) * BLOCK, :] = jnp.broadcast_to(
            jnp.where(ok > 0.5, 0.0, DEAD), (BLOCK, BLOCK)
        )

    def score(b, _):
        at = pl.multiple_of(b * BLOCK, BLOCK)
        s_ref[b] = mm_tn(row_ref[:, pl.ds(at, BLOCK)], tile_ref[b]) * SCALE
        return 0

    lax.fori_loop(0, row_blocks, score, 0, unroll=32)

    def score_lead(k, _):
        sl_ref[k] = mm_tn(lead_row_ref[k], lead_tile_ref[k]) * SCALE
        return 0

    lax.fori_loop(0, LEADS, score_lead, 0, unroll=8)

    parts[...] = jnp.zeros_like(parts)
    turn_ref[...] = jnp.zeros_like(turn_ref)
    prices[0] = price_ref[...]

    lane = lax.broadcasted_iota(jnp.int32, (BLOCK, BLOCK), 1)

    def place_of(k):
        places = idx_ref[2:3, 0:BLOCK]
        at = lax.broadcasted_iota(jnp.int32, (1, BLOCK), 1) == LEADS * LEAD_SLOTS + k
        return jnp.sum(jnp.where(at, places, 0), axis=1, keepdims=True)

    def price_rows(of_core, peer):
        return pl.ds(pl.multiple_of(of_core * half + peer * chunk, chunk), chunk)

    def row_copy(p, c, src, dst, peer, slot):
        rows = pl.ds(*CHUNKS[c])
        return pltpu.make_async_remote_copy(
            src_ref=src.at[p, rows],
            dst_ref=dst.at[p, slot, rows],
            send_sem=row_send.at[p, c, peer],
            recv_sem=row_recv.at[p, c, slot],
            device_id=(dp, peer),
            device_id_type=MESH,
        )

    def sib_copy(p, peer):
        return pltpu.make_async_remote_copy(
            src_ref=cols.at[p, price_rows(1 - core, peer)],
            dst_ref=sib_in.at[p, peer],
            send_sem=sib_send.at[p, peer],
            recv_sem=sib_recv.at[p, peer],
            device_id=(sibling, camp),
            device_id_type=MESH,
        )

    def z_copy(p, peer, slot):
        return pltpu.make_async_remote_copy(
            src_ref=z_out.at[p, peer],
            dst_ref=z_in.at[p, slot],
            send_sem=z_send.at[p, peer],
            recv_sem=z_recv.at[p, slot],
            device_id=(2 * peer + core, camp),
            device_id_type=MESH,
        )

    def price_copy(p, peer, owner):
        rows = price_rows(core, owner)
        return pltpu.make_async_remote_copy(
            src_ref=prices.at[p + 1, rows],
            dst_ref=prices.at[p + 1, rows],
            send_sem=pz_send.at[p, peer],
            recv_sem=pz_recv.at[p, owner],
            device_id=(2 * peer + core, camp),
            device_id_type=MESH,
        )

    def cross_copy(p, of_core, owner):
        rows = price_rows(of_core, owner)
        return pltpu.make_async_remote_copy(
            src_ref=prices.at[p + 1, rows],
            dst_ref=prices.at[p + 1, rows],
            send_sem=pc_send.at[p, owner],
            recv_sem=pc_recv.at[p, owner],
            device_id=(sibling, camp),
            device_id_type=MESH,
        )

    def drain(p):
        for c in range(chunks):
            for peer in camp_peers:
                row_copy(p, c, lse_ref, row_in, peer, camp).wait_send()
        for peer in z_peers:
            sib_copy(p, peer).wait_send()
            z_copy(p, peer, z).wait_send()
        sib_copy(p, z).wait_send()

    def drain_prices(p):
        for peer in z_peers:
            price_copy(p, peer, z).wait_send()
            cross_copy(p, core, peer).wait_send()
        cross_copy(p, core, z).wait_send()

    def one_pass(p, _):
        picked = exact_pick(selt[...], prices[p] * SCALE) + bias[...]
        pg[:, 0:BLOCK] = picked[0:row_blocks]
        pg[:, BLOCK : 2 * BLOCK] = picked[row_blocks : 2 * row_blocks]
        for s in range(LEAD_SLOTS):
            base = 2 * row_blocks + s * LEADS
            pgl[:, s * BLOCK : (s + 1) * BLOCK] = picked[base : base + LEADS]
        ml_ref[...] = jnp.zeros_like(ml_ref)
        ll_ref[...] = jnp.zeros_like(ll_ref)

        def visit_lead(k, _):
            place = place_of(k)
            price = pgl[pl.ds(k, 1), :]
            for r in range(0, BLOCK, 32):
                logit = sl_ref[k, r : r + 32, :] - price
                top = logit[:, 0:BLOCK]
                for s in range(1, LEAD_SLOTS):
                    top = jnp.maximum(top, logit[:, s * BLOCK : (s + 1) * BLOCK])
                m = jnp.maximum(jnp.max(top, axis=1, keepdims=True), 0.0)
                e = jnp.exp2(logit - m)
                el_ref[k, r : r + 32, :] = e
                total = e[:, 0:BLOCK]
                for s in range(1, LEAD_SLOTS):
                    total = total + e[:, s * BLOCK : (s + 1) * BLOCK]
                lead_sum_ref[k, r : r + 32, :] = total
                ml_ref[r : r + 32, :] = jnp.where(
                    lane[r : r + 32] == place, m, ml_ref[r : r + 32, :]
                )
            return 0

        lax.fori_loop(0, LEADS, visit_lead, 0, unroll=8)

        def add_lead(k, _):
            place = place_of(k)
            l = jnp.sum(lead_sum_ref[k], axis=1, keepdims=True)
            ll_ref[...] = jnp.where(lane == place, l, ll_ref[...])
            return 0

        lax.fori_loop(0, LEADS, add_lead, 0, unroll=8)
        m_ref[...] = ml_ref[...]

        def visit(c):
            start, size = CHUNKS[c]
            m_all = jnp.zeros((BLOCK, BLOCK), F32)
            l_all = jnp.zeros((BLOCK, BLOCK), F32)
            for u in range(size):
                b = start + u
                logit = s_ref[b] - pg[pl.ds(b, 1), :]
                top = jnp.maximum(logit[:, 0:BLOCK], logit[:, BLOCK:])
                m = jnp.maximum(jnp.max(top, axis=1, keepdims=True), 0.0)
                e = jnp.exp2(logit - m)
                e_ref[b] = e
                sum_ref[u] = e[:, 0:BLOCK] + e[:, BLOCK:]
                m_all = jnp.where(lane == b, m, m_all)
                if u >= 2:
                    l = jnp.sum(sum_ref[u - 2], axis=1, keepdims=True)
                    l_all = jnp.where(lane == b - 2, l, l_all)
            for u in range(size - 2, size):
                l = jnp.sum(sum_ref[u], axis=1, keepdims=True)
                l_all = jnp.where(lane == start + u, l, l_all)
            m_ref[...] = m_ref[...] + m_all
            l_all = l_all + ll_ref[...]
            l_ref[...] = (m_ref[...] + jnp.log2(jnp.maximum(l_all, 1e-37))).T
            rows = pl.ds(start, size)
            lse = l_ref[rows, :]
            lse_ref[p, rows, :] = lse
            row_in[p, camp, rows, :] = lse

            if c == 0:

                @pl.when(p == 0)
                def _():
                    pl.semaphore_wait(barrier, (n_camp - 1) + (n_z - 1) + 1)

            for peer in camp_peers:
                row_copy(p, c, lse_ref, row_in, peer, camp).start()

        for c in range(chunks):
            visit(c)

        @pl.when(p > 0)
        def _():
            drain_prices(p - 1)

        @pl.when(p == 0)
        def _():
            sel[...] = jnp.where(
                (lax.broadcasted_iota(jnp.int32, (col_blocks, wide), 0) == block_id)
                & (valid > 0),
                1.0,
                0.0,
            ).astype(BF16)

        def weigh(c):
            start, size = CHUNKS[c]
            rows = pl.ds(start, size)
            for peer in camp_peers[::-1]:
                row_copy(p, c, lse_ref, row_in, peer, peer).wait_recv()
            every = row_in[p, :, rows, :]
            top = jnp.maximum(jnp.max(every, axis=0), 0.0)
            total = jnp.exp2(-top) + jnp.sum(jnp.exp2(every - top[None]), axis=0)
            turn_ref[rows, :] = top + jnp.log2(total)
            weight = jnp.exp2(m_ref[...] - turn_ref[...].T)
            l_ref[...] = weight
            turned = pltpu.roll(weight, BLOCK - start, 1) if start else weight
            first, second = [], []
            whi = turned.astype(BF16)
            wmid = (turned - whi.astype(F32)).astype(BF16)
            terms = jnp.concatenate([whi, wmid], axis=1)
            pair = lax.rem(lax.broadcasted_iota(jnp.int32, (BLOCK, 2 * BLOCK), 1), BLOCK) // 2
            ri = lax.broadcasted_iota(jnp.int32, (2 * BLOCK, 2 * BLOCK), 0)
            ci = lax.broadcasted_iota(jnp.int32, (2 * BLOCK, 2 * BLOCK), 1)
            spread = jnp.where(lax.rem(ri, 2) == ci // BLOCK, 1.0, 0.0).astype(BF16)
            for u in range(0, size, 2):
                w2 = mm(jnp.where(pair == u // 2, terms, jnp.zeros_like(terms)), spread)
                for v in range(2):
                    w = w2[:, v * BLOCK : (v + 1) * BLOCK]
                    e = e_ref[start + u + v]
                    first.append(jnp.sum(e[:, 0:BLOCK] * w, axis=0, keepdims=True))
                    second.append(jnp.sum(e[:, BLOCK:] * w, axis=0, keepdims=True))
            parts[rows, :] = jnp.concatenate(first, axis=0)
            parts[pl.ds(row_blocks + start, size), :] = (
                jnp.concatenate(second, axis=0)
            )

        for c in range(chunks):
            weigh(c)

        def weigh_lead(k, _):
            place = place_of(k)
            w = jnp.sum(jnp.where(lane == place, l_ref[...], 0.0), axis=1, keepdims=True)
            part = jnp.sum(el_ref[k] * w, axis=0, keepdims=True)
            for s in range(LEAD_SLOTS):
                parts[pl.ds(2 * row_blocks + s * LEADS + k, 1), :] = part[
                    :, s * BLOCK : (s + 1) * BLOCK
                ]
            return 0

        for k in range(LEADS):
            weigh_lead(k, 0)

        terms = jnp.concatenate(pieces(parts[...]), axis=1)
        away = pl.ds(pl.multiple_of((1 - core) * half, half), half)
        home = pl.ds(pl.multiple_of(core * half, half), half)
        cols[p, away, :] = pick_terms(sel[away, :], terms)
        for peer in z_peers:
            sib_copy(p, peer).start()
        sib_copy(p, z).start()
        cols[p, home, :] = pick_terms(sel[home, :], terms)
        for peer in z_peers:
            sib_copy(p, peer).wait_recv()
            z_out[p, peer] = cols[p, price_rows(core, peer), :] + sib_in[p, peer]
            z_copy(p, peer, z).start()
        sib_copy(p, z).wait_recv()
        here = price_rows(core, z)
        total = cols[p, here, :] + sib_in[p, z]
        for peer in z_peers[::-1]:
            z_copy(p, peer, peer).wait_recv()
            total = total + z_in[p, peer]
        prices[p + 1, here, :] = jnp.maximum(
            prices[p, here, :] + step_ref[p] * (total - spend_ref[here, :]), 0.0
        )
        for peer in z_peers:
            price_copy(p, peer, z).start()
        cross_copy(p, core, z).start()
        drain(p)
        for peer in z_peers[::-1]:
            price_copy(p, peer, peer).wait_recv()
            cross_copy(p, core, peer).start()
        cross_copy(p, 1 - core, z).wait_recv()
        for peer in z_peers[::-1]:
            cross_copy(p, 1 - core, peer).wait_recv()
        return 0

    lax.fori_loop(0, PASSES, one_pass, 0)
    out_price[...] = prices[PASSES]
    out_norm[...] = turn_ref[0:row_blocks, :] * LN2

    drain_prices(PASSES - 1)


def local(
    n_dp, n_camp, row_factors, col_factors, prices, spend_target, step_sizes, eligible, counts
):
    row_blocks, slots = eligible.shape
    col_blocks = prices.shape[0] // BLOCK
    n_z = n_dp // 2
    side = math.isqrt(n_camp)
    chunk = col_blocks // 2 // n_z
    chunks = len(CHUNKS)
    wide = 256
    dma = pltpu.SemaphoreType.DMA
    vmem = pltpu.VMEM
    spec = pl.BlockSpec(memory_space=pltpu.VMEM)
    smem = pl.BlockSpec(memory_space=pltpu.SMEM)
    hbm = pl.BlockSpec(memory_space=pltpu.HBM)
    rows_t = row_factors.T
    index, tiles, lead_tiles, lead_rows = pl.pallas_call(
        functools.partial(gather_kernel, col_blocks),
        out_shape=(
            vmem((8, wide), jnp.int32),
            vmem((row_blocks, RANK, 2 * BLOCK), BF16),
            vmem((LEADS, RANK, LEAD_SLOTS * BLOCK), BF16),
            vmem((LEADS, RANK, BLOCK), BF16),
        ),
        in_specs=[hbm] * 4,
        out_specs=(spec,) * 4,
        scratch_shapes=[
            vmem((slots, row_blocks), jnp.int32),
            vmem((1, row_blocks), jnp.int32),
            vmem(rows_t.shape, BF16),
            vmem((RANK, col_blocks * BLOCK), BF16),
            pltpu.SMEM((8, wide), jnp.int32),
            dma((5,)),
        ],
        compiler_params=pltpu.CompilerParams(vmem_limit_bytes=60 * 1024 * 1024),
    )(eligible.T, counts.reshape(1, row_blocks), rows_t, col_factors.T)
    per_z = (PASSES, n_z, chunk, BLOCK)
    square = vmem((BLOCK, BLOCK), F32)
    new_prices, norms = pl.pallas_call(
        functools.partial(kernel, n_z, side),
        out_shape=(
            vmem((col_blocks, BLOCK), F32),
            vmem((row_blocks, BLOCK), F32),
        ),
        in_specs=[spec] * 6 + [smem, spec],
        out_specs=(spec, spec),
        scratch_shapes=[
            vmem((col_blocks, wide), BF16),
            vmem((wide, col_blocks), BF16),
            vmem((wide, BLOCK), F32),
            vmem((row_blocks, 2 * BLOCK), F32),
            vmem((LEADS, LEAD_SLOTS * BLOCK), F32),
            vmem((row_blocks, BLOCK, 2 * BLOCK), F32),
            vmem((LEADS, BLOCK, LEAD_SLOTS * BLOCK), F32),
            vmem((row_blocks, BLOCK, 2 * BLOCK), F32),
            vmem((LEADS, BLOCK, LEAD_SLOTS * BLOCK), F32),
            vmem((max(size for _, size in CHUNKS), BLOCK, BLOCK), F32),
            vmem((LEADS, BLOCK, BLOCK), F32),
            square,
            square,
            square,
            square,
            square,
            vmem((PASSES, row_blocks, BLOCK), F32),
            vmem((PASSES, n_camp, row_blocks, BLOCK), F32),
            vmem((wide, BLOCK), F32),
            vmem((PASSES, col_blocks, BLOCK), F32),
            vmem(per_z, F32),
            vmem(per_z, F32),
            vmem(per_z, F32),
            vmem((PASSES + 1, col_blocks, BLOCK), F32),
            dma((PASSES, chunks, n_camp)),
            dma((PASSES, chunks, n_camp)),
        ]
        + [dma((PASSES, n_z))] * 8,
        compiler_params=pltpu.CompilerParams(
            collective_id=0, has_side_effects=True, vmem_limit_bytes=48 * 1024 * 1024
        ),
    )(
        rows_t,
        tiles,
        lead_tiles,
        lead_rows,
        prices.reshape(col_blocks, BLOCK),
        spend_target.reshape(col_blocks, BLOCK),
        step_sizes,
        index,
    )
    return new_prices.reshape(-1), norms.reshape(-1)


def solution(mesh):
    placed = (P("dp", None), P("camp", None), P("camp"), P("camp"), P(), P("dp", None), P("dp"))
    return jax.shard_map(
        functools.partial(local, mesh.shape["dp"], mesh.shape["camp"]),
        mesh=mesh,
        in_specs=placed,
        out_specs=(P("camp"), P("dp")),
        check_vma=False,
    )
```
